32 devices in a mesh: step: 2 (over core), head: 4 (over z), blk: 4 (over y, x).
Axes of the slice: x: 2, y: 2, z: 4, core: 2. Of those that a mesh axis runs over, the one named last changes fastest.
Arguments:
- states: float32 [2, 256, 3072], P('step', ('head', 'blk')), may hold values from -6 to 6
- start: float32 [256, 3072], P(('head', 'blk')), may hold values from -6 to 6
- w_qkv: bfloat16 [3072, 3, 3072], P('blk', None, 'head'), may hold values from -0.109375 to 0.109375
- w_out: bfloat16 [3072, 3072], P(('head', 'blk')), may hold values from -0.109375 to 0.109375
- q_gain: float32 [64], replicated, may hold values from 1.5 to 5
- k_gain: float32 [64], replicated, may hold values from 1.5 to 5
- mod_table: float32 [50, 9216], replicated, may hold values from -3 to 3
- step_index: int32 [2], P('step'), may hold values from 0 to 49
- coef_table: float32 [50], replicated, may hold values from 0.1 to 1
- coef_index: int32 [2], P('step'), may hold values from 0 to 49
Outputs:
- new_states: float32 [2, 256, 3072], P('step', ('head', 'blk'))
The draws below stay inside these ranges and needn't reach their ends.
All inputs are finite; a program needn't handle non-finite values.
Results may differ from the reference program's by a relative error of at most 0.008.
Values may be sent and summed in bfloat16 or wider, within the bound.
A program may use at most 128 MiB of HBM per device.

```python
import math
import jax
import jax.numpy as jnp
from jax import lax

D = 3072
H = 48
HD = 64
TABLE = 50
STEPS = 2
L = 256


def draw_q_gain(key, part):
    key = jax.random.fold_in(key, 11)
    return jax.random.uniform(key, (HD,), jnp.float32, 1.5, 2.5)


def draw_k_gain(key, part):
    key = jax.random.fold_in(key, 23)
    return jax.random.uniform(key, (HD,), jnp.float32, 1.5, 2.5)


def block_levels(stream_key, shape, pieces, smallest, largest):
    def one(position, blocks):
        heights = jax.random.uniform(jax.random.fold_in(jax.random.fold_in(stream_key, 6), position), (blocks,), jnp.float32, smallest / len(pieces), largest / len(pieces))
        return jnp.repeat(jnp.exp(heights), shape[position] // blocks).reshape((-1,) + (1,) * (len(shape) - position - 1))

    gain = one(*pieces[0])
    for cut in pieces[1:]:
        gain = gain * one(*cut)
    return gain


def bell_draw(rng, extent, scale, most, shards=(), kind=jnp.bfloat16):
    level = block_levels(rng, extent, shards, -0.22, 0.18) if shards else 1.0
    entries = jax.random.normal(rng, extent, jnp.float32) * scale * level
    return jnp.minimum(jnp.maximum(entries, -most), most).astype(kind)


def setup_inputs(seed: int = 0) -> dict:
    splits = jax.random.split(jax.random.key(seed), 11)
    states = bell_draw(splits[0], (STEPS, L, D), 1.0, 6.0, ((0, 2), (1, 16)), jnp.float32)
    start = bell_draw(splits[1], (L, D), 1.0, 6.0, ((0, 16),), jnp.float32)
    w_qkv = bell_draw(splits[2], (D, 3, D), D ** -0.5, 0.109375, ((0, 4), (2, 4)))
    w_out = bell_draw(splits[3], (D, D), D ** -0.5, 0.109375, ((0, 16),))
    q_gain = draw_q_gain(jax.random.fold_in(splits[10], 71), 0)
    k_gain = draw_k_gain(jax.random.fold_in(splits[10], 71), 0)
    mod_table = bell_draw(splits[6], (TABLE, 3 * D), 0.5, 3.0, (), jnp.float32)
    step_index = jax.random.randint(splits[7], (STEPS,), 0, TABLE).astype(jnp.int32)
    coef_table = jnp.clip(jnp.exp(jax.random.uniform(splits[8], (TABLE,), jnp.float32, math.log(0.1), math.log(1.0))), 0.1, 1.0)
    coef_index = jax.random.randint(splits[9], (STEPS,), 0, TABLE).astype(jnp.int32)
    return dict(states=states, start=start, w_qkv=w_qkv, w_out=w_out, q_gain=q_gain, k_gain=k_gain, mod_table=mod_table, step_index=step_index, coef_table=coef_table, coef_index=coef_index)


def head_norm(values_in, gains):
    middle = lax.optimization_barrier(jnp.mean(values_in, axis=-1, keepdims=True))
    spread = lax.optimization_barrier(jnp.mean((values_in - middle) ** 2, axis=-1, keepdims=True))
    return (values_in - middle) * lax.rsqrt(spread + 1e-06) * gains

def reference(states, start, w_qkv, w_out, q_gain, k_gain, mod_table, step_index, coef_table, coef_index):
    modulation = mod_table[step_index].reshape(STEPS, 3, D)
    coefs = coef_table[coef_index]

    def one_step(packed):
        current, mods = packed
        middle = lax.optimization_barrier(jnp.mean(current, axis=-1, keepdims=True))
        spread = lax.optimization_barrier(jnp.mean((current - middle) ** 2, axis=-1, keepdims=True))
        normed = ((current - middle) * lax.rsqrt(spread + 1e-05) * (1.0 + mods[1]) + mods[0]).astype(jnp.bfloat16)
        projected = jnp.dot(normed, w_qkv.reshape(D, 3 * D), preferred_element_type=jnp.float32).reshape(L, 3, H, HD)
        queries = head_norm(projected[:, 0], q_gain).astype(jnp.bfloat16)
        keys_all = head_norm(projected[:, 1], k_gain).astype(jnp.bfloat16)
        values_all = projected[:, 2].astype(jnp.bfloat16)
        scores = jnp.einsum('qhd,khd->hqk', queries.astype(jnp.float32), keys_all.astype(jnp.float32)) * HD ** (-0.5)
        peak = lax.optimization_barrier(jnp.max(scores, axis=-1, keepdims=True))
        weights = jnp.exp(scores - peak)
        totals = lax.optimization_barrier(jnp.sum(weights, axis=-1))
        mixed = jnp.einsum('hqk,khd->qhd', weights.astype(jnp.bfloat16).astype(jnp.float32), values_all.astype(jnp.float32))
        mixed = mixed / jnp.transpose(totals)[:, :, None]
        attn = mixed.reshape(L, D).astype(jnp.bfloat16)
        return mods[2] * jnp.dot(attn, w_out, preferred_element_type=jnp.float32)
    drifts = lax.map(one_step, (states, modulation))
    return start[None] + jnp.cumsum(coefs[:, None, None] * drifts, axis=0)
```

```python
import functools

import jax
import jax.numpy as jnp
from jax import lax
from jax.experimental import pallas as pl
from jax.experimental.pallas import tpu as pltpu
from jax.sharding import PartitionSpec as P

HD = 64
MESH = pl.DeviceIdType.MESH


def carried_in(array, axis, join, neutral):
    place = lax.axis_index(axis)
    gathered = lax.all_gather(array.astype(jnp.bfloat16), axis)
    state = jnp.zeros_like(array) + jnp.asarray(neutral, array.dtype)

    def one(step, state):
        return join(state, lax.dynamic_index_in_dim(gathered, step, 0, False).astype(array.dtype))

    return lax.fori_loop(0, place, one, state)


def head_norm(values_in, gains):
    middle = jnp.mean(values_in, axis=-1, keepdims=True)
    spread = jnp.mean((values_in - middle) ** 2, axis=-1, keepdims=True)
    return (values_in - middle) * lax.rsqrt(spread + 1e-06) * gains


def general_plan(
    states, start, w_qkv, w_out, q_gain, k_gain, mod_table, step_index, coef_table, coef_index
):
    width = states.shape[2]
    table_size = mod_table.shape[0]
    slot_ids = jnp.arange(table_size, dtype=jnp.int32)[None, :]
    mod_picks = (step_index[:, None] == slot_ids).astype(jnp.float32)
    coef_picks = (coef_index[:, None] == slot_ids).astype(jnp.float32)
    modulation = jnp.dot(mod_picks, mod_table, precision=lax.Precision.HIGHEST).reshape(
        -1, 3, width
    )
    coefs = jnp.sum(coef_picks * coef_table[None, :], axis=1)
    middle = jnp.mean(states, axis=-1, keepdims=True)
    spread = jnp.mean((states - middle) ** 2, axis=-1, keepdims=True)
    normed = (
        (states - middle) * lax.rsqrt(spread + 1e-05) * (1.0 + modulation[:, 1][:, None, :])
        + modulation[:, 0][:, None, :]
    ).astype(jnp.bfloat16)
    weight_rows = lax.all_gather(w_qkv, "blk", axis=0, tiled=True)
    projected = jnp.einsum(
        "std,dce->stce",
        lax.all_gather(normed, "head", axis=1, tiled=True),
        weight_rows,
        preferred_element_type=jnp.float32,
    )
    step_count = projected.shape[0]
    row_count = projected.shape[1]
    local_heads = projected.shape[3] // HD
    queries = head_norm(
        projected[:, :, 0].reshape(step_count, row_count, local_heads, HD), q_gain
    ).astype(jnp.bfloat16)
    keys_here = head_norm(
        projected[:, :, 1].reshape(step_count, row_count, local_heads, HD), k_gain
    ).astype(jnp.bfloat16)
    values_here = (
        projected[:, :, 2].reshape(step_count, row_count, local_heads, HD).astype(jnp.bfloat16)
    )
    scale_factor = HD ** (-0.5)
    start_best = jnp.full((step_count, local_heads, row_count), -1e30, jnp.float32)
    start_totals = jnp.zeros((step_count, local_heads, row_count), jnp.float32)
    start_accum = jnp.zeros((step_count, local_heads, row_count, HD), jnp.float32)
    best = start_best
    totals = start_totals
    accum = start_accum
    key_piece = lax.all_gather(keys_here, "blk", axis=1, tiled=True)
    value_piece = lax.all_gather(values_here, "blk", axis=1, tiled=True)
    length = key_piece.shape[1]
    for offset in range(0, length, 512):
        stop = min(offset + 512, length)
        key_block = key_piece[:, offset:stop]
        value_block = value_piece[:, offset:stop]
        scores = (
            jnp.einsum("sqhd,skhd->shqk", queries, key_block, preferred_element_type=jnp.float32)
            * scale_factor
        )
        new_best = jnp.maximum(best, jnp.max(scores, axis=-1))
        factor = jnp.exp(best - new_best)
        weights = jnp.exp(scores - new_best[..., None])
        totals = totals * factor + jnp.sum(weights, axis=-1)
        accum = accum * factor[..., None] + jnp.einsum(
            "shqk,skhd->shqd",
            weights.astype(jnp.bfloat16),
            value_block,
            preferred_element_type=jnp.float32,
        )
        best = new_best
    best, totals, accum = (best, totals, accum)
    attn = jnp.transpose(accum / totals[..., None], (0, 2, 1, 3)).reshape(
        step_count, row_count, local_heads * HD
    )
    attn = attn.astype(jnp.bfloat16)
    group_terms = jnp.einsum(
        "srf,fe->sre",
        attn,
        lax.all_gather(w_out, "blk", axis=0, tiled=True),
        preferred_element_type=jnp.float32,
    )
    mixed = lax.psum_scatter(
        group_terms.astype(jnp.bfloat16), "head", scatter_dimension=1, tiled=True
    ).astype(jnp.float32)
    drift = modulation[:, 2][:, None, :] * mixed
    inclusive = jnp.cumsum(coefs[:, None, None] * drift, axis=0)
    own_total = inclusive[-1]
    earlier = carried_in(
        own_total, "step", lambda first, second: first + second, jnp.zeros_like(own_total)
    )
    return start[None] + (earlier[None] + inclusive)


def paired(place, turn):
    bit = 1
    while bit <= turn:
        if turn & bit:
            place = place + bit * (1 - 2 * ((place // bit) % 2))
        bit *= 2
    return place


def whole_kernel(
    sizes,
    states_ref, start_ref, w_qkv_ref, w_out_ref, q_gain_ref, k_gain_ref, mod_ref,
    step_index_ref, coef_table_ref, coef_index_ref,
    out_ref,
    w_buf, mod_buf, norm_send, norm_got, part_send, part_got, attn_buf, wo_buf,
    out_send, out_got, carry_send, carry_got, q_buf, k_buf, v_buf,
    local_sem, norm_ss, norm_rs, part_ss, part_rs, attn_ss, attn_rs,
    wo_ss, wo_rs, fwd_ss, fwd_rs, out_ss, out_rs, carry_ss, carry_rs,
):
    nh, nb = sizes
    n = nh * nb
    rows, width = start_ref.shape
    depth = w_buf.shape[1]
    own_cols = w_buf.shape[2] // nb
    out_cols = width // nb
    half = own_cols // 2
    local_heads = own_cols // HD
    group_rows = nb * rows
    step = lax.axis_index("step")
    head = lax.axis_index("head")
    blk = lax.axis_index("blk")
    me = head * nb + blk

    mod_copy = pltpu.make_async_copy(mod_ref, mod_buf, local_sem.at[0])
    mod_copy.start()
    w_copy = pltpu.make_async_copy(w_qkv_ref, w_buf, local_sem.at[1])
    w_copy.start()
    wo_copy = pltpu.make_async_copy(
        w_out_ref.at[:, pl.ds(pl.multiple_of(blk * out_cols, 128), out_cols)],
        wo_buf.at[blk],
        local_sem.at[2],
    )
    wo_copy.start()

    barrier = pltpu.get_barrier_semaphore()
    for d in range(1, n):
        other = (me + d) % n
        pl.semaphore_signal(
            barrier, inc=1, device_id=(step, other // nb, other % nb), device_id_type=MESH
        )
    pl.semaphore_signal(barrier, inc=1, device_id=(1 - step, head, blk), device_id_type=MESH)

    current = states_ref[0]
    middle = jnp.mean(current, axis=-1, keepdims=True)
    spread = jnp.mean((current - middle) ** 2, axis=-1, keepdims=True)
    mod_copy.wait()
    slot = step_index_ref[0]
    shift = mod_buf[pl.ds(slot, 1), 0:width]
    scale = mod_buf[pl.ds(slot, 1), width : 2 * width]
    normed = (
        (current - middle) * lax.rsqrt(spread + 1e-05) * (1.0 + scale) + shift
    ).astype(jnp.bfloat16)
    for c in range(nb):
        norm_send[c] = normed[:, c * depth : (c + 1) * depth]
    norm_got[me] = norm_send[blk]
    pl.semaphore_wait(barrier, n)

    def norm_copy(i, j):
        there_h, there_b = paired(head, i), (blk + j) % nb
        return pltpu.make_async_remote_copy(
            src_ref=norm_send.at[there_b],
            dst_ref=norm_got.at[me],
            send_sem=norm_ss.at[i * nb + j],
            recv_sem=norm_rs.at[me],
            device_id=(step, there_h, there_b),
            device_id_type=MESH,
        )

    def norm_arrival(i, j):
        source = paired(head, i) * nb + (blk + j) % nb
        return pltpu.make_async_remote_copy(
            src_ref=norm_send.at[0],
            dst_ref=norm_got.at[source],
            send_sem=norm_ss.at[0],
            recv_sem=norm_rs.at[source],
            device_id=(step, head, blk),
            device_id_type=MESH,
        )

    others = [(i, j) for i in range(nh) for j in range(nb) if i or j]
    for i, j in others:
        norm_copy(i, j).start()

    def wo_send(e):
        there = (blk + e) % nb
        return pltpu.make_async_remote_copy(
            src_ref=w_out_ref.at[
                pl.ds(pl.multiple_of(step * half, 16), half),
                pl.ds(pl.multiple_of(there * out_cols, 128), out_cols),
            ],
            dst_ref=wo_buf.at[blk, pl.ds(pl.multiple_of(step * half, 16), half)],
            send_sem=wo_ss.at[e],
            recv_sem=wo_rs.at[blk],
            device_id=(step, head, there),
            device_id_type=MESH,
        )

    def wo_half(source, which, sems, rsems, e):
        place = wo_buf.at[source, pl.ds(pl.multiple_of(which * half, 16), half)]
        return pltpu.make_async_remote_copy(
            src_ref=place,
            dst_ref=place,
            send_sem=sems.at[e],
            recv_sem=rsems.at[source],
            device_id=(1 - step, head, blk),
            device_id_type=MESH,
        )

    for e in range(1, nb):
        wo_send(e).start()

    def part_copy(i, e):
        there = (blk + e) % nb
        return pltpu.make_async_remote_copy(
            src_ref=part_send.at[i, there],
            dst_ref=part_got.at[i, blk],
            send_sem=part_ss.at[i * nb + e],
            recv_sem=part_rs.at[i * nb + blk],
            device_id=(step, head, there),
            device_id_type=MESH,
        )

    def part_arrival(i, e):
        source = (blk + e) % nb
        return pltpu.make_async_remote_copy(
            src_ref=part_send.at[i, 0],
            dst_ref=part_got.at[i, source],
            send_sem=part_ss.at[0],
            recv_sem=part_rs.at[i * nb + source],
            device_id=(step, head, blk),
            device_id_type=MESH,
        )

    w_copy.wait()
    for i in range(nh):
        for j in range(nb):
            if i or j:
                norm_arrival(i, j).wait_recv()
        first = pl.multiple_of(paired(head, i) * nb, nb)
        tokens = norm_got[pl.ds(first, nb)].reshape(group_rows, depth)
        terms = [
            jnp.dot(tokens, w_buf[c], preferred_element_type=jnp.float32).astype(jnp.bfloat16)
            for c in range(3)
        ]
        for c in range(nb):
            part_send[i, c] = jnp.concatenate(
                [term[:, c * own_cols : (c + 1) * own_cols] for term in terms], axis=1
            )
        for e in range(1, nb):
            part_copy(i, e).start()

    for e in range(1, nb):
        source = (blk + e) % nb
        wo_half(source, step, wo_ss, wo_rs, 0).wait_recv()
        wo_half(source, step, fwd_ss, fwd_rs, e).start()

    def head_parts(values, gains):
        center = jnp.mean(values, axis=-1, keepdims=True)
        width_sq = jnp.mean((values - center) ** 2, axis=-1, keepdims=True)
        return (values - center) * lax.rsqrt(width_sq + 1e-06) * gains

    for i in range(nh):
        total = part_send[i, blk].astype(jnp.float32)
        for e in range(1, nb):
            part_arrival(i, e).wait_recv()
            total = total + part_got[i, (blk + e) % nb].astype(jnp.float32)
        here = slice(i * group_rows, (i + 1) * group_rows)
        for g in range(local_heads):
            at = g * HD
            q_buf[g, here] = head_parts(total[:, at : at + HD], q_gain_ref[...]).astype(
                jnp.bfloat16
            )
            at += own_cols
            k_buf[g, here] = head_parts(total[:, at : at + HD], k_gain_ref[...]).astype(
                jnp.bfloat16
            )
            at += own_cols
            v_buf[g, here] = total[:, at : at + HD].astype(jnp.bfloat16)

    mixed = []
    for g in range(local_heads):
        scores = lax.dot_general(
            q_buf[g], k_buf[g], (((1,), (1,)), ((), ())), preferred_element_type=jnp.float32
        ) * (HD ** (-0.5))
        weights = jnp.exp(scores - jnp.max(scores, axis=-1, keepdims=True))
        totals = jnp.sum(weights, axis=-1, keepdims=True)
        value = jnp.dot(
            weights.astype(jnp.bfloat16), v_buf[g], preferred_element_type=jnp.float32
        )
        mixed.append((value / totals).astype(jnp.bfloat16))
    attn_buf[blk] = jnp.concatenate(mixed, axis=1)

    def attn_copy(e):
        there = (blk + e) % nb
        return pltpu.make_async_remote_copy(
            src_ref=attn_buf.at[blk],
            dst_ref=attn_buf.at[blk],
            send_sem=attn_ss.at[e],
            recv_sem=attn_rs.at[blk],
            device_id=(step, head, there),
            device_id_type=MESH,
        )

    def attn_arrival(e):
        source = (blk + e) % nb
        return pltpu.make_async_remote_copy(
            src_ref=attn_buf.at[blk],
            dst_ref=attn_buf.at[source],
            send_sem=attn_ss.at[0],
            recv_sem=attn_rs.at[source],
            device_id=(step, head, blk),
            device_id_type=MESH,
        )

    for e in range(1, nb):
        attn_copy(e).start()

    wo_copy.wait()
    for e in range(1, nb):
        source = (blk + e) % nb
        wo_half(source, 1 - step, fwd_ss, fwd_rs, 0).wait_recv()
    for e in range(1, nb):
        attn_arrival(e).wait_recv()

    def out_copy(i, j):
        return pltpu.make_async_remote_copy(
            src_ref=out_send.at[i * nb + j],
            dst_ref=out_got.at[me],
            send_sem=out_ss.at[i * nb + j],
            recv_sem=out_rs.at[me],
            device_id=(step, paired(head, i), j),
            device_id_type=MESH,
        )

    def out_arrival(source):
        return pltpu.make_async_remote_copy(
            src_ref=out_send.at[0],
            dst_ref=out_got.at[source],
            send_sem=out_ss.at[0],
            recv_sem=out_rs.at[source],
            device_id=(step, head, blk),
            device_id_type=MESH,
        )

    for i in reversed(range(nh)):
        here = slice(i * group_rows, (i + 1) * group_rows)
        drift = jnp.dot(attn_buf[0, here], wo_buf[0], preferred_element_type=jnp.float32)
        for c in range(1, nb):
            drift = drift + jnp.dot(
                attn_buf[c, here], wo_buf[c], preferred_element_type=jnp.float32
            )
        out_send[i * nb : (i + 1) * nb] = drift.astype(jnp.bfloat16).reshape(nb, rows, out_cols)
        for j in range(nb):
            if i:
                out_copy(i, j).start()
            else:
                @pl.when(j != blk)
                def _():
                    out_copy(i, j).start()
    out_got[me] = out_send[blk]

    coef = coef_table_ref[coef_index_ref[0]]
    for i, j in others:
        out_arrival(paired(head, i) * nb + (blk + j) % nb).wait_recv()

    moved = []
    for c in range(nb):
        total = out_got[c].astype(jnp.float32)
        for h in range(1, nh):
            total = total + out_got[h * nb + c].astype(jnp.float32)
        gate = mod_buf[
            pl.ds(slot, 1), 2 * width + c * out_cols : 2 * width + (c + 1) * out_cols
        ]
        moved.append(coef * (gate * total))

    carry = pltpu.make_async_remote_copy(
        src_ref=carry_send,
        dst_ref=carry_got,
        send_sem=carry_ss.at[0],
        recv_sem=carry_rs.at[0],
        device_id=(1 - step, head, blk),
        device_id_type=MESH,
    )

    @pl.when(step == 0)
    def _():
        for c in range(nb):
            carry_send[:, c * out_cols : (c + 1) * out_cols] = moved[c].astype(jnp.bfloat16)
        carry.start()
        for c in range(nb):
            cols = slice(c * out_cols, (c + 1) * out_cols)
            out_ref[0, :, cols] = start_ref[:, cols] + moved[c]

    @pl.when(step == 1)
    def _():
        carry.wait_recv()
        for c in range(nb):
            cols = slice(c * out_cols, (c + 1) * out_cols)
            out_ref[0, :, cols] = start_ref[:, cols] + (
                carry_got[:, cols].astype(jnp.float32) + moved[c]
            )

    for i, j in others:
        norm_copy(i, j).wait_send()
    for e in range(1, nb):
        wo_send(e).wait_send()
        wo_half((blk + e) % nb, step, fwd_ss, fwd_rs, e).wait_send()
        attn_copy(e).wait_send()
        for i in range(nh):
            part_copy(i, e).wait_send()
    for i in range(nh):
        for j in range(nb):
            if i:
                out_copy(i, j).wait_send()
            else:
                @pl.when(j != blk)
                def _():
                    out_copy(i, j).wait_send()

    @pl.when(step == 0)
    def _():
        carry.wait_send()


def one_kernel(
    sizes,
    states, start, w_qkv, w_out, q_gain, k_gain, mod_table, step_index, coef_table, coef_index
):
    nh, nb = sizes
    n = nh * nb
    rows, width = start.shape
    depth, _, cols = w_qkv.shape
    own_cols = cols // nb
    out_cols = width // nb
    local_heads = own_cols // HD
    length = rows * n
    half16 = jnp.bfloat16
    vmem = pl.BlockSpec(memory_space=pltpu.VMEM)
    smem = pl.BlockSpec(memory_space=pltpu.SMEM)
    hbm = pl.BlockSpec(memory_space=pl.ANY)
    dma = pltpu.SemaphoreType.DMA
    return pl.pallas_call(
        functools.partial(whole_kernel, sizes),
        out_shape=jax.ShapeDtypeStruct(states.shape, jnp.float32),
        in_specs=[vmem, vmem, hbm, hbm, vmem, vmem, hbm, smem, smem, smem],
        out_specs=vmem,
        scratch_shapes=[
            pltpu.VMEM((3, depth, cols), half16),
            pltpu.VMEM(mod_table.shape, jnp.float32),
            pltpu.VMEM((nb, rows, depth), half16),
            pltpu.VMEM((n, rows, depth), half16),
            pltpu.VMEM((nh, nb, nb * rows, 3 * own_cols), half16),
            pltpu.VMEM((nh, nb, nb * rows, 3 * own_cols), half16),
            pltpu.VMEM((nb, length, own_cols), half16),
            pltpu.VMEM((nb, own_cols, out_cols), half16),
            pltpu.VMEM((n, rows, out_cols), half16),
            pltpu.VMEM((n, rows, out_cols), half16),
            pltpu.VMEM((rows, width), half16),
            pltpu.VMEM((rows, width), half16),
            pltpu.VMEM((local_heads, length, HD), half16),
            pltpu.VMEM((local_heads, length, HD), half16),
            pltpu.VMEM((local_heads, length, HD), half16),
            dma((3,)),
            dma((n,)), dma((n,)),
            dma((n,)), dma((n,)),
            dma((nb,)), dma((nb,)),
            dma((nb,)), dma((nb,)),
            dma((nb,)), dma((nb,)),
            dma((n,)), dma((n,)),
            dma((1,)), dma((1,)),
        ],
        compiler_params=pltpu.CompilerParams(
            collective_id=0, has_side_effects=True, vmem_limit_bytes=48 * 1024 * 1024
        ),
        name="picard_step",
    )(
        states, start, jnp.transpose(w_qkv, (1, 0, 2)), w_out,
        q_gain[None], k_gain[None], mod_table, step_index, coef_table, coef_index,
    )


def on_device(sizes, *arrays):
    step_count, nh, nb = sizes
    states, start, w_qkv, w_out = arrays[:4]
    rows, width = start.shape
    depth, _, cols = w_qkv.shape
    fits = (
        step_count == 2
        and states.shape[0] == 1
        and nh & (nh - 1) == 0
        and rows % 16 == 0
        and cols % (nb * HD) == 0
        and w_out.shape[0] == cols // nb
        and (cols // nb) % 32 == 0
        and depth * nb == width
        and depth % 128 == 0
    )
    if fits:
        return one_kernel((nh, nb), *arrays)
    return general_plan(*arrays)


def solution(mesh):
    in_specs = (
        P("step", ("head", "blk"), None),
        P(("head", "blk"), None),
        P("blk", None, "head"),
        P(("head", "blk"), None),
        P(),
        P(),
        P(),
        P("step"),
        P(),
        P("step"),
    )
    out_specs = P("step", ("head", "blk"), None)
    sizes = (mesh.shape["step"], mesh.shape["head"], mesh.shape["blk"])
    return jax.shard_map(
        functools.partial(on_device, sizes), mesh=mesh, in_specs=in_specs, out_specs=out_specs, check_vma=False
    )
```

```python
import functools

import jax
import jax.numpy as jnp
from jax import lax
from jax.experimental import pallas as pl
from jax.experimental.pallas import tpu as pltpu
from jax.sharding import PartitionSpec as P

HD = 64
MESH = pl.DeviceIdType.MESH


def carried_in(array, axis, join, neutral):
    place = lax.axis_index(axis)
    gathered = lax.all_gather(array.astype(jnp.bfloat16), axis)
    state = jnp.zeros_like(array) + jnp.asarray(neutral, array.dtype)

    def one(step, state):
        return join(state, lax.dynamic_index_in_dim(gathered, step, 0, False).astype(array.dtype))

    return lax.fori_loop(0, place, one, state)


def head_norm(values_in, gains):
    middle = jnp.mean(values_in, axis=-1, keepdims=True)
    spread = jnp.mean((values_in - middle) ** 2, axis=-1, keepdims=True)
    return (values_in - middle) * lax.rsqrt(spread + 1e-06) * gains


def general_plan(
    states, start, w_qkv, w_out, q_gain, k_gain, mod_table, step_index, coef_table, coef_index
):
    width = states.shape[2]
    table_size = mod_table.shape[0]
    slot_ids = jnp.arange(table_size, dtype=jnp.int32)[None, :]
    mod_picks = (step_index[:, None] == slot_ids).astype(jnp.float32)
    coef_picks = (coef_index[:, None] == slot_ids).astype(jnp.float32)
    modulation = jnp.dot(mod_picks, mod_table, precision=lax.Precision.HIGHEST).reshape(
        -1, 3, width
    )
    coefs = jnp.sum(coef_picks * coef_table[None, :], axis=1)
    middle = jnp.mean(states, axis=-1, keepdims=True)
    spread = jnp.mean((states - middle) ** 2, axis=-1, keepdims=True)
    normed = (
        (states - middle) * lax.rsqrt(spread + 1e-05) * (1.0 + modulation[:, 1][:, None, :])
        + modulation[:, 0][:, None, :]
    ).astype(jnp.bfloat16)
    weight_rows = lax.all_gather(w_qkv, "blk", axis=0, tiled=True)
    projected = jnp.einsum(
        "std,dce->stce",
        lax.all_gather(normed, "head", axis=1, tiled=True),
        weight_rows,
        preferred_element_type=jnp.float32,
    )
    step_count = projected.shape[0]
    row_count = projected.shape[1]
    local_heads = projected.shape[3] // HD
    queries = head_norm(
        projected[:, :, 0].reshape(step_count, row_count, local_heads, HD), q_gain
    ).astype(jnp.bfloat16)
    keys_here = head_norm(
        projected[:, :, 1].reshape(step_count, row_count, local_heads, HD), k_gain
    ).astype(jnp.bfloat16)
    values_here = (
        projected[:, :, 2].reshape(step_count, row_count, local_heads, HD).astype(jnp.bfloat16)
    )
    scale_factor = HD ** (-0.5)
    start_best = jnp.full((step_count, local_heads, row_count), -1e30, jnp.float32)
    start_totals = jnp.zeros((step_count, local_heads, row_count), jnp.float32)
    start_accum = jnp.zeros((step_count, local_heads, row_count, HD), jnp.float32)
    best = start_best
    totals = start_totals
    accum = start_accum
    key_piece = lax.all_gather(keys_here, "blk", axis=1, tiled=True)
    value_piece = lax.all_gather(values_here, "blk", axis=1, tiled=True)
    length = key_piece.shape[1]
    for offset in range(0, length, 512):
        stop = min(offset + 512, length)
        key_block = key_piece[:, offset:stop]
        value_block = value_piece[:, offset:stop]
        scores = (
            jnp.einsum("sqhd,skhd->shqk", queries, key_block, preferred_element_type=jnp.float32)
            * scale_factor
        )
        new_best = jnp.maximum(best, jnp.max(scores, axis=-1))
        factor = jnp.exp(best - new_best)
        weights = jnp.exp(scores - new_best[..., None])
        totals = totals * factor + jnp.sum(weights, axis=-1)
        accum = accum * factor[..., None] + jnp.einsum(
            "shqk,skhd->shqd",
            weights.astype(jnp.bfloat16),
            value_block,
            preferred_element_type=jnp.float32,
        )
        best = new_best
    best, totals, accum = (best, totals, accum)
    attn = jnp.transpose(accum / totals[..., None], (0, 2, 1, 3)).reshape(
        step_count, row_count, local_heads * HD
    )
    attn = attn.astype(jnp.bfloat16)
    group_terms = jnp.einsum(
        "srf,fe->sre",
        attn,
        lax.all_gather(w_out, "blk", axis=0, tiled=True),
        preferred_element_type=jnp.float32,
    )
    mixed = lax.psum_scatter(
        group_terms.astype(jnp.bfloat16), "head", scatter_dimension=1, tiled=True
    ).astype(jnp.float32)
    drift = modulation[:, 2][:, None, :] * mixed
    inclusive = jnp.cumsum(coefs[:, None, None] * drift, axis=0)
    own_total = inclusive[-1]
    earlier = carried_in(
        own_total, "step", lambda first, second: first + second, jnp.zeros_like(own_total)
    )
    return start[None] + (earlier[None] + inclusive)


def paired(place, turn):
    bit = 1
    while bit <= turn:
        if turn & bit:
            place = place + bit * (1 - 2 * ((place // bit) % 2))
        bit *= 2
    return place


def pack(values):
    rows, cols = values.shape
    tiles = [values[:, at : at + 128] for at in range(0, cols - 127, 128)]
    if cols % 128:
        rest = values[:, cols - 64 :]
        tiles.append(jnp.concatenate([rest[: rows // 2], rest[rows // 2 :]], axis=1))
    return tiles


def unpack(buffer, rows, cols):
    full = cols // 128
    parts = [buffer[t * rows : (t + 1) * rows] for t in range(full)]
    if cols % 128:
        rest = buffer[full * rows :]
        parts.append(jnp.concatenate([rest[:, :64], rest[:, 64:]], axis=0))
    return jnp.concatenate(parts, axis=1)


def whole_kernel(
    sizes,
    states_hbm, start_hbm, w_qkv_ref, w_out_ref, q_gain_hbm, k_gain_hbm, mod_ref,
    step_index_hbm, coef_table_hbm, coef_index_hbm,
    out_ref,
    states_ref, start_ref, q_gain_ref, k_gain_ref, step_index_ref, coef_table_ref, coef_index_ref,
    w_buf, mod_buf, norm_send, norm_got, part_send, part_got, part_own, attn_buf, wo_buf,
    out_send, out_got, carry_send, carry_got, q_buf, k_buf, v_buf,
    local_sem, norm_ss, norm_rs, part_ss, part_rs, attn_ss, attn_rs,
    wo_ss, wo_rs, fwd_ss, fwd_rs, out_ss, out_rs, carry_ss, carry_rs,
):
    nh, nb = sizes
    n = nh * nb
    rows, width = start_ref.shape
    depth = w_buf.shape[1]
    own_cols = w_buf.shape[2] // nb
    out_cols = width // nb
    half = own_cols // 2
    local_heads = own_cols // HD
    group_rows = nb * rows
    step = lax.axis_index("step")
    head = lax.axis_index("head")
    blk = lax.axis_index("blk")
    me = head * nb + blk

    fetches = [
        pltpu.make_async_copy(source, target, local_sem.at[3 + place])
        for place, (source, target) in enumerate(
            (
                (states_hbm, states_ref),
                (step_index_hbm, step_index_ref),
                (q_gain_hbm, q_gain_ref),
                (k_gain_hbm, k_gain_ref),
                (coef_index_hbm, coef_index_ref),
                (coef_table_hbm, coef_table_ref),
                (start_hbm, start_ref),
            )
        )
    ]
    for fetch in fetches[:2]:
        fetch.start()
    mod_copy = pltpu.make_async_copy(mod_ref, mod_buf, local_sem.at[0])
    mod_copy.start()
    for fetch in fetches[2:]:
        fetch.start()
    w_copy = pltpu.make_async_copy(w_qkv_ref, w_buf, local_sem.at[1])
    w_copy.start()
    wo_copy = pltpu.make_async_copy(
        w_out_ref.at[:, pl.ds(pl.multiple_of(blk * out_cols, 128), out_cols)],
        wo_buf.at[blk],
        local_sem.at[2],
    )
    wo_copy.start()

    barrier = pltpu.get_barrier_semaphore()
    for d in range(1, n):
        other = (me + d) % n
        pl.semaphore_signal(
            barrier, inc=1, device_id=(step, other // nb, other % nb), device_id_type=MESH
        )
    pl.semaphore_signal(barrier, inc=1, device_id=(1 - step, head, blk), device_id_type=MESH)

    fetches[0].wait()
    current = states_ref[0]
    middle = jnp.mean(current, axis=-1, keepdims=True)
    spread = jnp.mean((current - middle) ** 2, axis=-1, keepdims=True)
    fetches[1].wait()
    mod_copy.wait()
    slot = step_index_ref[0]
    shift = mod_buf[pl.ds(slot, 1), 0:width]
    scale = mod_buf[pl.ds(slot, 1), width : 2 * width]
    normed = (
        (current - middle) * lax.rsqrt(spread + 1e-05) * (1.0 + scale) + shift
    ).astype(jnp.bfloat16)
    for c in range(nb):
        norm_send[c] = normed[:, c * depth : (c + 1) * depth]
    norm_got[me] = norm_send[blk]
    pl.semaphore_wait(barrier, n)

    def norm_copy(i, j):
        there_h, there_b = paired(head, i), (blk + j) % nb
        return pltpu.make_async_remote_copy(
            src_ref=norm_send.at[there_b],
            dst_ref=norm_got.at[me],
            send_sem=norm_ss.at[i * nb + j],
            recv_sem=norm_rs.at[me],
            device_id=(step, there_h, there_b),
            device_id_type=MESH,
        )

    def norm_arrival(i, j):
        source = paired(head, i) * nb + (blk + j) % nb
        return pltpu.make_async_remote_copy(
            src_ref=norm_send.at[0],
            dst_ref=norm_got.at[source],
            send_sem=norm_ss.at[0],
            recv_sem=norm_rs.at[source],
            device_id=(step, head, blk),
            device_id_type=MESH,
        )

    others = [(i, j) for i in range(nh) for j in range(nb) if i or j]
    for i, j in others:
        norm_copy(i, j).start()

    def wo_send(e):
        there = (blk + e) % nb
        return pltpu.make_async_remote_copy(
            src_ref=w_out_ref.at[
                pl.ds(pl.multiple_of(step * half, 16), half),
                pl.ds(pl.multiple_of(there * out_cols, 128), out_cols),
            ],
            dst_ref=wo_buf.at[blk, pl.ds(pl.multiple_of(step * half, 16), half)],
            send_sem=wo_ss.at[e],
            recv_sem=wo_rs.at[blk],
            device_id=(step, head, there),
            device_id_type=MESH,
        )

    def wo_half(source, which, sems, rsems, e):
        place = wo_buf.at[source, pl.ds(pl.multiple_of(which * half, 16), half)]
        return pltpu.make_async_remote_copy(
            src_ref=place,
            dst_ref=place,
            send_sem=sems.at[e],
            recv_sem=rsems.at[source],
            device_id=(1 - step, head, blk),
            device_id_type=MESH,
        )

    for e in range(1, nb):
        wo_send(e).start()

    def part_copy(i, e):
        there = (blk + e) % nb
        return pltpu.make_async_remote_copy(
            src_ref=part_send.at[i, there],
            dst_ref=part_got.at[i, blk],
            send_sem=part_ss.at[i * nb + e],
            recv_sem=part_rs.at[i * nb + blk],
            device_id=(step, head, there),
            device_id_type=MESH,
        )

    def part_arrival(i, e):
        source = (blk + e) % nb
        return pltpu.make_async_remote_copy(
            src_ref=part_send.at[i, 0],
            dst_ref=part_got.at[i, source],
            send_sem=part_ss.at[0],
            recv_sem=part_rs.at[i * nb + source],
            device_id=(step, head, blk),
            device_id_type=MESH,
        )

    w_copy.wait()
    for i in range(nh):
        for j in range(nb):
            if i or j:
                norm_arrival(i, j).wait_recv()
        first = pl.multiple_of(paired(head, i) * nb, nb)
        tokens = norm_got[pl.ds(first, nb)].reshape(group_rows, depth)
        terms = [
            jnp.dot(tokens, w_buf[c], preferred_element_type=jnp.float32) for c in range(3)
        ]
        for c in range(nb):
            share = jnp.concatenate(
                [term[:, c * own_cols : (c + 1) * own_cols] for term in terms], axis=1
            )

            @pl.when(blk == c)
            def _():
                part_own[i] = share

            @pl.when(blk != c)
            def _():
                packed = pack(share.astype(jnp.bfloat16))
                for t, tile in enumerate(packed):
                    part_send[i, c, t * group_rows : t * group_rows + tile.shape[0]] = tile

        for e in range(1, nb):
            part_copy(i, e).start()

    for e in range(1, nb):
        source = (blk + e) % nb
        wo_half(source, step, wo_ss, wo_rs, 0).wait_recv()
        wo_half(source, step, fwd_ss, fwd_rs, e).start()

    def head_parts(values, gains):
        center = jnp.mean(values, axis=-1, keepdims=True)
        width_sq = jnp.mean((values - center) ** 2, axis=-1, keepdims=True)
        return (values - center) * lax.rsqrt(width_sq + 1e-06) * gains

    fetches[2].wait()
    fetches[3].wait()
    for i in range(nh):
        total = part_own[i]
        for e in range(1, nb):
            part_arrival(i, e).wait_recv()
            total = total + unpack(
                part_got[i, (blk + e) % nb], group_rows, 3 * own_cols
            ).astype(jnp.float32)
        here = slice(i * group_rows, (i + 1) * group_rows)
        for g in range(local_heads):
            at = g * HD
            q_buf[g, here] = head_parts(total[:, at : at + HD], q_gain_ref[...]).astype(
                jnp.bfloat16
            )
            at += own_cols
            k_buf[g, here] = head_parts(total[:, at : at + HD], k_gain_ref[...]).astype(
                jnp.bfloat16
            )
            at += own_cols
            v_buf[g, here] = total[:, at : at + HD].astype(jnp.bfloat16)

    def attn_copy(s, e):
        there = (blk + e) % nb
        return pltpu.make_async_remote_copy(
            src_ref=attn_buf.at[s, blk],
            dst_ref=attn_buf.at[s, blk],
            send_sem=attn_ss.at[s * nb + e],
            recv_sem=attn_rs.at[s * nb + blk],
            device_id=(step, head, there),
            device_id_type=MESH,
        )

    def attn_arrival(s, e):
        source = (blk + e) % nb
        return pltpu.make_async_remote_copy(
            src_ref=attn_buf.at[s, blk],
            dst_ref=attn_buf.at[s, source],
            send_sem=attn_ss.at[0],
            recv_sem=attn_rs.at[s * nb + source],
            device_id=(step, head, blk),
            device_id_type=MESH,
        )

    pair_rows = 2 * group_rows
    pairs = list(reversed(range(nh // 2)))
    for s in pairs:
        here = slice(s * pair_rows, (s + 1) * pair_rows)
        mixed = []
        for g in range(local_heads):
            scores = lax.dot_general(
                q_buf[g, here],
                k_buf[g],
                (((1,), (1,)), ((), ())),
                preferred_element_type=jnp.float32,
            ) * (HD ** (-0.5))
            weights = jnp.exp(scores - jnp.max(scores, axis=-1, keepdims=True))
            totals = jnp.sum(weights, axis=-1, keepdims=True)
            value = jnp.dot(
                weights.astype(jnp.bfloat16), v_buf[g], preferred_element_type=jnp.float32
            )
            mixed.append((value / totals).astype(jnp.bfloat16))
        for t, tile in enumerate(pack(jnp.concatenate(mixed, axis=1))):
            attn_buf[s, blk, t * pair_rows : t * pair_rows + tile.shape[0]] = tile
        for e in range(1, nb):
            attn_copy(s, e).start()

    wo_copy.wait()
    for e in range(1, nb):
        source = (blk + e) % nb
        wo_half(source, 1 - step, fwd_ss, fwd_rs, 0).wait_recv()

    def out_copy(i, j):
        return pltpu.make_async_remote_copy(
            src_ref=out_send.at[i * nb + j],
            dst_ref=out_got.at[me],
            send_sem=out_ss.at[i * nb + j],
            recv_sem=out_rs.at[me],
            device_id=(step, paired(head, i), j),
            device_id_type=MESH,
        )

    def out_arrival(source):
        return pltpu.make_async_remote_copy(
            src_ref=out_send.at[0],
            dst_ref=out_got.at[source],
            send_sem=out_ss.at[0],
            recv_sem=out_rs.at[source],
            device_id=(step, head, blk),
            device_id_type=MESH,
        )

    for s in pairs:
        drift = jnp.dot(
            unpack(attn_buf[s, blk], pair_rows, own_cols),
            wo_buf[blk],
            preferred_element_type=jnp.float32,
        )
        for e in range(1, nb):
            source = (blk + e) % nb
            attn_arrival(s, e).wait_recv()
            drift = drift + jnp.dot(
                unpack(attn_buf[s, source], pair_rows, own_cols),
                wo_buf[source],
                preferred_element_type=jnp.float32,
            )
        out_send[2 * s * nb : 2 * (s + 1) * nb] = drift.astype(jnp.bfloat16).reshape(
            2 * nb, rows, out_cols
        )
        for i in (2 * s + 1, 2 * s):
            for j in range(nb):
                if i:
                    out_copy(i, j).start()
                else:
                    @pl.when(j != blk)
                    def _():
                        out_copy(i, j).start()
    out_got[me] = out_send[blk]

    for fetch in fetches[4:]:
        fetch.wait()
    coef = coef_table_ref[coef_index_ref[0]]
    for i, j in others:
        out_arrival(paired(head, i) * nb + (blk + j) % nb).wait_recv()

    moved = []
    for c in range(nb):
        total = out_got[c].astype(jnp.float32)
        for h in range(1, nh):
            total = total + out_got[h * nb + c].astype(jnp.float32)
        gate = mod_buf[
            pl.ds(slot, 1), 2 * width + c * out_cols : 2 * width + (c + 1) * out_cols
        ]
        moved.append(coef * (gate * total))

    carry = pltpu.make_async_remote_copy(
        src_ref=carry_send,
        dst_ref=carry_got,
        send_sem=carry_ss.at[0],
        recv_sem=carry_rs.at[0],
        device_id=(1 - step, head, blk),
        device_id_type=MESH,
    )

    @pl.when(step == 0)
    def _():
        for c in range(nb):
            carry_send[:, c * out_cols : (c + 1) * out_cols] = moved[c].astype(jnp.bfloat16)
        carry.start()
        for c in range(nb):
            cols = slice(c * out_cols, (c + 1) * out_cols)
            out_ref[0, :, cols] = start_ref[:, cols] + moved[c]

    @pl.when(step == 1)
    def _():
        carry.wait_recv()
        for c in range(nb):
            cols = slice(c * out_cols, (c + 1) * out_cols)
            out_ref[0, :, cols] = start_ref[:, cols] + (
                carry_got[:, cols].astype(jnp.float32) + moved[c]
            )

    for i, j in others:
        norm_copy(i, j).wait_send()
    for e in range(1, nb):
        wo_send(e).wait_send()
        wo_half((blk + e) % nb, step, fwd_ss, fwd_rs, e).wait_send()
        for s in pairs:
            attn_copy(s, e).wait_send()
        for i in range(nh):
            part_copy(i, e).wait_send()
    for i in range(nh):
        for j in range(nb):
            if i:
                out_copy(i, j).wait_send()
            else:
                @pl.when(j != blk)
                def _():
                    out_copy(i, j).wait_send()

    @pl.when(step == 0)
    def _():
        carry.wait_send()


def one_kernel(
    sizes,
    states, start, w_qkv, w_out, q_gain, k_gain, mod_table, step_index, coef_table, coef_index
):
    nh, nb = sizes
    n = nh * nb
    rows, width = start.shape
    depth, _, cols = w_qkv.shape
    own_cols = cols // nb
    out_cols = width // nb
    local_heads = own_cols // HD
    length = rows * n
    half16 = jnp.bfloat16
    vmem = pl.BlockSpec(memory_space=pltpu.VMEM)
    hbm = pl.BlockSpec(memory_space=pltpu.HBM)
    dma = pltpu.SemaphoreType.DMA
    return pl.pallas_call(
        functools.partial(whole_kernel, sizes),
        out_shape=jax.ShapeDtypeStruct(states.shape, jnp.float32),
        in_specs=[hbm] * 10,
        out_specs=vmem,
        scratch_shapes=[
            pltpu.VMEM(states.shape, jnp.float32),
            pltpu.VMEM(start.shape, jnp.float32),
            pltpu.VMEM((1, HD), jnp.float32),
            pltpu.VMEM((1, HD), jnp.float32),
            pltpu.SMEM(step_index.shape, jnp.int32),
            pltpu.SMEM(coef_table.shape, jnp.float32),
            pltpu.SMEM(coef_index.shape, jnp.int32),
            pltpu.VMEM((3, depth, cols), half16),
            pltpu.VMEM(mod_table.shape, jnp.float32),
            pltpu.VMEM((nb, rows, depth), half16),
            pltpu.VMEM((n, rows, depth), half16),
            pltpu.VMEM((nh, nb, nb * rows * 3 * own_cols // 128, 128), half16),
            pltpu.VMEM((nh, nb, nb * rows * 3 * own_cols // 128, 128), half16),
            pltpu.VMEM((nh, nb * rows, 3 * own_cols), jnp.float32),
            pltpu.VMEM((nh // 2, nb, 2 * nb * rows * own_cols // 128, 128), half16),
            pltpu.VMEM((nb, own_cols, out_cols), half16),
            pltpu.VMEM((n, rows, out_cols), half16),
            pltpu.VMEM((n, rows, out_cols), half16),
            pltpu.VMEM((rows, width), half16),
            pltpu.VMEM((rows, width), half16),
            pltpu.VMEM((local_heads, length, HD), half16),
            pltpu.VMEM((local_heads, length, HD), half16),
            pltpu.VMEM((local_heads, length, HD), half16),
            dma((10,)),
            dma((n,)), dma((n,)),
            dma((n,)), dma((n,)),
            dma((nb * nh // 2,)), dma((nb * nh // 2,)),
            dma((nb,)), dma((nb,)),
            dma((nb,)), dma((nb,)),
            dma((n,)), dma((n,)),
            dma((1,)), dma((1,)),
        ],
        compiler_params=pltpu.CompilerParams(
            collective_id=0, has_side_effects=True, vmem_limit_bytes=32 * 1024 * 1024
        ),
        name="picard_step",
    )(
        states, start, jnp.transpose(w_qkv, (1, 0, 2)), w_out,
        q_gain[None], k_gain[None], mod_table, step_index, coef_table, coef_index,
    )


def on_device(sizes, *arrays):
    step_count, nh, nb = sizes
    states, start, w_qkv, w_out = arrays[:4]
    rows, width = start.shape
    depth, _, cols = w_qkv.shape
    fits = (
        step_count == 2
        and states.shape[0] == 1
        and nh % 2 == 0
        and nh & (nh - 1) == 0
        and rows % 16 == 0
        and cols % (nb * HD) == 0
        and w_out.shape[0] == cols // nb
        and (cols // nb) % 32 == 0
        and depth * nb == width
        and depth % 128 == 0
    )
    if fits:
        return one_kernel((nh, nb), *arrays)
    return general_plan(*arrays)


def solution(mesh):
    in_specs = (
        P("step", ("head", "blk"), None),
        P(("head", "blk"), None),
        P("blk", None, "head"),
        P(("head", "blk"), None),
        P(),
        P(),
        P(),
        P("step"),
        P(),
        P("step"),
    )
    out_specs = P("step", ("head", "blk"), None)
    sizes = (mesh.shape["step"], mesh.shape["head"], mesh.shape["blk"])
    return jax.shard_map(
        functools.partial(on_device, sizes), mesh=mesh, in_specs=in_specs, out_specs=out_specs, check_vma=False
    )
```

```python
import functools

import jax
import jax.numpy as jnp
from jax import lax
from jax.experimental import pallas as pl
from jax.experimental.pallas import tpu as pltpu
from jax.sharding import PartitionSpec as P

HD = 64
MESH = pl.DeviceIdType.MESH


def carried_in(array, axis, join, neutral):
    place = lax.axis_index(axis)
    gathered = lax.all_gather(array.astype(jnp.bfloat16), axis)
    state = jnp.zeros_like(array) + jnp.asarray(neutral, array.dtype)

    def one(step, state):
        return join(state, lax.dynamic_index_in_dim(gathered, step, 0, False).astype(array.dtype))

    return lax.fori_loop(0, place, one, state)


def head_norm(values_in, gains):
    middle = jnp.mean(values_in, axis=-1, keepdims=True)
    spread = jnp.mean((values_in - middle) ** 2, axis=-1, keepdims=True)
    return (values_in - middle) * lax.rsqrt(spread + 1e-06) * gains


def general_plan(
    states, start, w_qkv, w_out, q_gain, k_gain, mod_table, step_index, coef_table, coef_index
):
    width = states.shape[2]
    table_size = mod_table.shape[0]
    slot_ids = jnp.arange(table_size, dtype=jnp.int32)[None, :]
    mod_picks = (step_index[:, None] == slot_ids).astype(jnp.float32)
    coef_picks = (coef_index[:, None] == slot_ids).astype(jnp.float32)
    modulation = jnp.dot(mod_picks, mod_table, precision=lax.Precision.HIGHEST).reshape(
        -1, 3, width
    )
    coefs = jnp.sum(coef_picks * coef_table[None, :], axis=1)
    middle = jnp.mean(states, axis=-1, keepdims=True)
    spread = jnp.mean((states - middle) ** 2, axis=-1, keepdims=True)
    normed = (
        (states - middle) * lax.rsqrt(spread + 1e-05) * (1.0 + modulation[:, 1][:, None, :])
        + modulation[:, 0][:, None, :]
    ).astype(jnp.bfloat16)
    weight_rows = lax.all_gather(w_qkv, "blk", axis=0, tiled=True)
    projected = jnp.einsum(
        "std,dce->stce",
        lax.all_gather(normed, "head", axis=1, tiled=True),
        weight_rows,
        preferred_element_type=jnp.float32,
    )
    step_count = projected.shape[0]
    row_count = projected.shape[1]
    local_heads = projected.shape[3] // HD
    queries = head_norm(
        projected[:, :, 0].reshape(step_count, row_count, local_heads, HD), q_gain
    ).astype(jnp.bfloat16)
    keys_here = head_norm(
        projected[:, :, 1].reshape(step_count, row_count, local_heads, HD), k_gain
    ).astype(jnp.bfloat16)
    values_here = (
        projected[:, :, 2].reshape(step_count, row_count, local_heads, HD).astype(jnp.bfloat16)
    )
    scale_factor = HD ** (-0.5)
    start_best = jnp.full((step_count, local_heads, row_count), -1e30, jnp.float32)
    start_totals = jnp.zeros((step_count, local_heads, row_count), jnp.float32)
    start_accum = jnp.zeros((step_count, local_heads, row_count, HD), jnp.float32)
    best = start_best
    totals = start_totals
    accum = start_accum
    key_piece = lax.all_gather(keys_here, "blk", axis=1, tiled=True)
    value_piece = lax.all_gather(values_here, "blk", axis=1, tiled=True)
    length = key_piece.shape[1]
    for offset in range(0, length, 512):
        stop = min(offset + 512, length)
        key_block = key_piece[:, offset:stop]
        value_block = value_piece[:, offset:stop]
        scores = (
            jnp.einsum("sqhd,skhd->shqk", queries, key_block, preferred_element_type=jnp.float32)
            * scale_factor
        )
        new_best = jnp.maximum(best, jnp.max(scores, axis=-1))
        factor = jnp.exp(best - new_best)
        weights = jnp.exp(scores - new_best[..., None])
        totals = totals * factor + jnp.sum(weights, axis=-1)
        accum = accum * factor[..., None] + jnp.einsum(
            "shqk,skhd->shqd",
            weights.astype(jnp.bfloat16),
            value_block,
            preferred_element_type=jnp.float32,
        )
        best = new_best
    best, totals, accum = (best, totals, accum)
    attn = jnp.transpose(accum / totals[..., None], (0, 2, 1, 3)).reshape(
        step_count, row_count, local_heads * HD
    )
    attn = attn.astype(jnp.bfloat16)
    group_terms = jnp.einsum(
        "srf,fe->sre",
        attn,
        lax.all_gather(w_out, "blk", axis=0, tiled=True),
        preferred_element_type=jnp.float32,
    )
    mixed = lax.psum_scatter(
        group_terms.astype(jnp.bfloat16), "head", scatter_dimension=1, tiled=True
    ).astype(jnp.float32)
    drift = modulation[:, 2][:, None, :] * mixed
    inclusive = jnp.cumsum(coefs[:, None, None] * drift, axis=0)
    own_total = inclusive[-1]
    earlier = carried_in(
        own_total, "step", lambda first, second: first + second, jnp.zeros_like(own_total)
    )
    return start[None] + (earlier[None] + inclusive)


def paired(place, turn):
    bit = 1
    while bit <= turn:
        if turn & bit:
            place = place + bit * (1 - 2 * ((place // bit) % 2))
        bit *= 2
    return place


def pack(values):
    rows, cols = values.shape
    tiles = [values[:, at : at + 128] for at in range(0, cols - 127, 128)]
    if cols % 128:
        rest = values[:, cols - 64 :]
        tiles.append(jnp.concatenate([rest[: rows // 2], rest[rows // 2 :]], axis=1))
    return tiles


def unpack(buffer, rows, cols):
    full = cols // 128
    parts = [buffer[t * rows : (t + 1) * rows] for t in range(full)]
    if cols % 128:
        rest = buffer[full * rows :]
        parts.append(jnp.concatenate([rest[:, :64], rest[:, 64:]], axis=0))
    return jnp.concatenate(parts, axis=1)


def whole_kernel(
    sizes,
    states_hbm, start_hbm, w_qkv_ref, w_out_ref, q_gain_hbm, k_gain_hbm, mod_ref,
    step_index_hbm, coef_table_hbm, coef_index_hbm,
    out_ref,
    states_ref, start_ref, q_gain_ref, k_gain_ref, step_index_ref, coef_table_ref, coef_index_ref,
    w_buf, mod_buf, norm_send, norm_got, part_send, part_got, part_own, attn_buf, wo_buf,
    out_send, out_got, carry_send, carry_got, q_buf, k_buf, v_buf,
    local_sem, norm_ss, norm_rs, relay_ss, relay_rs, part_ss, part_rs, attn_ss, attn_rs,
    wo_ss, wo_rs, fwd_ss, fwd_rs, out_ss, out_rs, carry_ss, carry_rs,
):
    nh, nb = sizes
    n = nh * nb
    rows, width = start_ref.shape
    depth = w_buf.shape[1]
    own_cols = w_buf.shape[2] // nb
    out_cols = width // nb
    half = own_cols // 2
    local_heads = own_cols // HD
    group_rows = nb * rows
    step = lax.axis_index("step")
    head = lax.axis_index("head")
    blk = lax.axis_index("blk")
    me = head * nb + blk

    fetches = [
        pltpu.make_async_copy(source, target, local_sem.at[3 + place])
        for place, (source, target) in enumerate(
            (
                (states_hbm, states_ref),
                (step_index_hbm, step_index_ref),
                (q_gain_hbm, q_gain_ref),
                (k_gain_hbm, k_gain_ref),
                (coef_index_hbm, coef_index_ref),
                (coef_table_hbm, coef_table_ref),
                (start_hbm, start_ref),
            )
        )
    ]
    for fetch in fetches[:2]:
        fetch.start()
    mod_copy = pltpu.make_async_copy(mod_ref, mod_buf, local_sem.at[0])
    mod_copy.start()
    for fetch in fetches[2:]:
        fetch.start()
    w_copy = pltpu.make_async_copy(w_qkv_ref, w_buf, local_sem.at[1])
    w_copy.start()
    wo_copy = pltpu.make_async_copy(
        w_out_ref.at[:, pl.ds(pl.multiple_of(blk * out_cols, 128), out_cols)],
        wo_buf.at[blk],
        local_sem.at[2],
    )
    wo_copy.start()

    barrier = pltpu.get_barrier_semaphore()
    for e in range(1, nb):
        pl.semaphore_signal(
            barrier, inc=1, device_id=(step, head, (blk + e) % nb), device_id_type=MESH
        )
    pl.semaphore_signal(barrier, inc=1, device_id=(1 - step, head, blk), device_id_type=MESH)

    @pl.when(head > 0)
    def _():
        pl.semaphore_signal(barrier, inc=1, device_id=(step, head - 1, blk), device_id_type=MESH)

    @pl.when(head < nh - 1)
    def _():
        pl.semaphore_signal(barrier, inc=1, device_id=(step, head + 1, blk), device_id_type=MESH)

    fetches[0].wait()
    current = states_ref[0]
    middle = jnp.mean(current, axis=-1, keepdims=True)
    spread = jnp.mean((current - middle) ** 2, axis=-1, keepdims=True)
    fetches[1].wait()
    mod_copy.wait()
    slot = step_index_ref[0]
    shift = mod_buf[pl.ds(slot, 1), 0:width]
    scale = mod_buf[pl.ds(slot, 1), width : 2 * width]
    normed = (
        (current - middle) * lax.rsqrt(spread + 1e-05) * (1.0 + scale) + shift
    ).astype(jnp.bfloat16)
    for c in range(nb):
        norm_send[c] = normed[:, c * depth : (c + 1) * depth]
    norm_got[me] = norm_send[blk]
    pl.semaphore_wait(barrier, nb + jnp.minimum(head, 1) + jnp.minimum(nh - 1 - head, 1))

    def norm_copy(e):
        there = (blk + e) % nb
        return pltpu.make_async_remote_copy(
            src_ref=norm_send.at[there],
            dst_ref=norm_got.at[me],
            send_sem=norm_ss.at[e],
            recv_sem=norm_rs.at[blk],
            device_id=(step, head, there),
            device_id_type=MESH,
        )

    def norm_arrival(e):
        source = (blk + e) % nb
        return pltpu.make_async_remote_copy(
            src_ref=norm_send.at[0],
            dst_ref=norm_got.at[head * nb + source],
            send_sem=norm_ss.at[0],
            recv_sem=norm_rs.at[source],
            device_id=(step, head, blk),
            device_id_type=MESH,
        )

    def relay(origin, way):
        place = norm_got.at[pl.ds(origin * nb, nb)]
        return pltpu.make_async_remote_copy(
            src_ref=place,
            dst_ref=place,
            send_sem=relay_ss.at[way * nh + origin],
            recv_sem=relay_rs.at[origin],
            device_id=(step, head + 1 - 2 * way, blk),
            device_id_type=MESH,
        )

    def upward(origin):
        @pl.when(head < nh - 1)
        def _():
            relay(origin, 0).start()

    def downward(origin):
        @pl.when(head > 0)
        def _():
            relay(origin, 1).start()

    for e in range(1, nb):
        norm_copy(e).start()

    def wo_send(e):
        there = (blk + e) % nb
        return pltpu.make_async_remote_copy(
            src_ref=w_out_ref.at[
                pl.ds(pl.multiple_of(step * half, 16), half),
                pl.ds(pl.multiple_of(there * out_cols, 128), out_cols),
            ],
            dst_ref=wo_buf.at[blk, pl.ds(pl.multiple_of(step * half, 16), half)],
            send_sem=wo_ss.at[e],
            recv_sem=wo_rs.at[blk],
            device_id=(step, head, there),
            device_id_type=MESH,
        )

    def wo_half(source, which, sems, rsems, e):
        place = wo_buf.at[source, pl.ds(pl.multiple_of(which * half, 16), half)]
        return pltpu.make_async_remote_copy(
            src_ref=place,
            dst_ref=place,
            send_sem=sems.at[e],
            recv_sem=rsems.at[source],
            device_id=(1 - step, head, blk),
            device_id_type=MESH,
        )

    for e in range(1, nb):
        wo_send(e).start()

    def part_copy(i, e):
        there = (blk + e) % nb
        return pltpu.make_async_remote_copy(
            src_ref=part_send.at[i, there],
            dst_ref=part_got.at[i, blk],
            send_sem=part_ss.at[i * nb + e],
            recv_sem=part_rs.at[i * nb + blk],
            device_id=(step, head, there),
            device_id_type=MESH,
        )

    def part_arrival(i, e):
        source = (blk + e) % nb
        return pltpu.make_async_remote_copy(
            src_ref=part_send.at[i, 0],
            dst_ref=part_got.at[i, source],
            send_sem=part_ss.at[0],
            recv_sem=part_rs.at[i * nb + source],
            device_id=(step, head, blk),
            device_id_type=MESH,
        )

    for e in range(1, nb):
        norm_arrival(e).wait_recv()
    upward(head)
    downward(head)
    w_copy.wait()

    def project(i):
        tokens = norm_got[pl.ds(i * nb, nb)].reshape(group_rows, depth)
        terms = [
            jnp.dot(tokens, w_buf[c], preferred_element_type=jnp.float32) for c in range(3)
        ]
        for c in range(nb):
            share = jnp.concatenate(
                [term[:, c * own_cols : (c + 1) * own_cols] for term in terms], axis=1
            )

            @pl.when(blk == c)
            def _():
                part_own[i] = share

            @pl.when(blk != c)
            def _():
                packed = pack(share.astype(jnp.bfloat16))
                for t, tile in enumerate(packed):
                    part_send[i, c, t * group_rows : t * group_rows + tile.shape[0]] = tile

        for e in range(1, nb):
            part_copy(i, e).start()

    project(head)

    def further(d, carried):
        low, high = head - d, head + d

        @pl.when(low >= 0)
        def _():
            relay(low, 0).wait_recv()
            upward(low)

        @pl.when(high < nh)
        def _():
            relay(high, 0).wait_recv()
            downward(high)

        @pl.when(low >= 0)
        def _():
            project(low)

        @pl.when(high < nh)
        def _():
            project(high)

        return carried

    lax.fori_loop(1, nh, further, 0)

    for e in range(1, nb):
        source = (blk + e) % nb
        wo_half(source, step, wo_ss, wo_rs, 0).wait_recv()
        wo_half(source, step, fwd_ss, fwd_rs, e).start()

    def head_parts(values, gains):
        center = jnp.mean(values, axis=-1, keepdims=True)
        width_sq = jnp.mean((values - center) ** 2, axis=-1, keepdims=True)
        return (values - center) * lax.rsqrt(width_sq + 1e-06) * gains

    fetches[2].wait()
    fetches[3].wait()

    def finish(i, carried):
        total = part_own[i]
        for e in range(1, nb):
            part_arrival(i, e).wait_recv()
            total = total + unpack(
                part_got.at[i, (blk + e) % nb], group_rows, 3 * own_cols
            ).astype(jnp.float32)
        here = pl.ds(pl.multiple_of(i * group_rows, group_rows), group_rows)
        for g in range(local_heads):
            at = g * HD
            q_buf[g, here] = head_parts(total[:, at : at + HD], q_gain_ref[...]).astype(
                jnp.bfloat16
            )
            at += own_cols
            k_buf[g, here] = head_parts(total[:, at : at + HD], k_gain_ref[...]).astype(
                jnp.bfloat16
            )
            at += own_cols
            v_buf[g, here] = total[:, at : at + HD].astype(jnp.bfloat16)
        return carried

    for i in range(nh):
        finish(paired(head, i), 0)

    def attn_copy(s, e):
        there = (blk + e) % nb
        return pltpu.make_async_remote_copy(
            src_ref=attn_buf.at[s, blk],
            dst_ref=attn_buf.at[s, blk],
            send_sem=attn_ss.at[s * nb + e],
            recv_sem=attn_rs.at[s * nb + blk],
            device_id=(step, head, there),
            device_id_type=MESH,
        )

    def attn_arrival(s, e):
        source = (blk + e) % nb
        return pltpu.make_async_remote_copy(
            src_ref=attn_buf.at[s, blk],
            dst_ref=attn_buf.at[s, source],
            send_sem=attn_ss.at[0],
            recv_sem=attn_rs.at[s * nb + source],
            device_id=(step, head, blk),
            device_id_type=MESH,
        )

    pair_rows = 2 * group_rows
    pairs = list(reversed(range(nh // 2)))
    for s in pairs:
        here = slice(s * pair_rows, (s + 1) * pair_rows)
        mixed = []
        for g in range(local_heads):
            scores = lax.dot_general(
                q_buf[g, here],
                k_buf[g],
                (((1,), (1,)), ((), ())),
                preferred_element_type=jnp.float32,
            ) * (HD ** (-0.5))
            weights = jnp.exp(scores - jnp.max(scores, axis=-1, keepdims=True))
            totals = jnp.sum(weights, axis=-1, keepdims=True)
            value = jnp.dot(
                weights.astype(jnp.bfloat16), v_buf[g], preferred_element_type=jnp.float32
            )
            mixed.append((value / totals).astype(jnp.bfloat16))
        for t, tile in enumerate(pack(jnp.concatenate(mixed, axis=1))):
            attn_buf[s, blk, t * pair_rows : t * pair_rows + tile.shape[0]] = tile
        for e in range(1, nb):
            attn_copy(s, e).start()

    wo_copy.wait()
    for e in range(1, nb):
        source = (blk + e) % nb
        wo_half(source, 1 - step, fwd_ss, fwd_rs, 0).wait_recv()

    def out_copy(i, j):
        return pltpu.make_async_remote_copy(
            src_ref=out_send.at[i * nb + j],
            dst_ref=out_got.at[me],
            send_sem=out_ss.at[i * nb + j],
            recv_sem=out_rs.at[me],
            device_id=(step, i, j),
            device_id_type=MESH,
        )

    def out_arrival(source):
        return pltpu.make_async_remote_copy(
            src_ref=out_send.at[0],
            dst_ref=out_got.at[source],
            send_sem=out_ss.at[0],
            recv_sem=out_rs.at[source],
            device_id=(step, head, blk),
            device_id_type=MESH,
        )

    for s in pairs:
        drift = jnp.dot(
            unpack(attn_buf[s, blk], pair_rows, own_cols),
            wo_buf[blk],
            preferred_element_type=jnp.float32,
        )
        for e in range(1, nb):
            source = (blk + e) % nb
            attn_arrival(s, e).wait_recv()
            drift = drift + jnp.dot(
                unpack(attn_buf[s, source], pair_rows, own_cols),
                wo_buf[source],
                preferred_element_type=jnp.float32,
            )
        out_send[2 * s * nb : 2 * (s + 1) * nb] = drift.astype(jnp.bfloat16).reshape(
            2 * nb, rows, out_cols
        )
        for i in (2 * s, 2 * s + 1):
            for j in range(nb):
                @pl.when((head != i) | (blk != j))
                def _():
                    out_copy(i, j).start()
    out_got[me] = out_send[me]

    for fetch in fetches[4:]:
        fetch.wait()
    coef = coef_table_ref[coef_index_ref[0]]
    for d in range(1, n):
        out_arrival((me + d) % n).wait_recv()

    moved = []
    for c in range(nb):
        total = out_got[c].astype(jnp.float32)
        for h in range(1, nh):
            total = total + out_got[h * nb + c].astype(jnp.float32)
        gate = mod_buf[
            pl.ds(slot, 1), 2 * width + c * out_cols : 2 * width + (c + 1) * out_cols
        ]
        moved.append(coef * (gate * total))

    carry = pltpu.make_async_remote_copy(
        src_ref=carry_send,
        dst_ref=carry_got,
        send_sem=carry_ss.at[0],
        recv_sem=carry_rs.at[0],
        device_id=(1 - step, head, blk),
        device_id_type=MESH,
    )

    @pl.when(step == 0)
    def _():
        for c in range(nb):
            carry_send[:, c * out_cols : (c + 1) * out_cols] = moved[c].astype(jnp.bfloat16)
        carry.start()
        for c in range(nb):
            cols = slice(c * out_cols, (c + 1) * out_cols)
            out_ref[0, :, cols] = start_ref[:, cols] + moved[c]

    @pl.when(step == 1)
    def _():
        carry.wait_recv()
        for c in range(nb):
            cols = slice(c * out_cols, (c + 1) * out_cols)
            out_ref[0, :, cols] = start_ref[:, cols] + (
                carry_got[:, cols].astype(jnp.float32) + moved[c]
            )

    for i in range(nh):
        @pl.when((i <= head) & (head < nh - 1))
        def _():
            relay(i, 0).wait_send()

        @pl.when((i >= head) & (head > 0))
        def _():
            relay(i, 1).wait_send()

    for e in range(1, nb):
        norm_copy(e).wait_send()
        wo_send(e).wait_send()
        wo_half((blk + e) % nb, step, fwd_ss, fwd_rs, e).wait_send()
        for s in pairs:
            attn_copy(s, e).wait_send()
        for i in range(nh):
            part_copy(i, e).wait_send()
    for i in range(nh):
        for j in range(nb):
            @pl.when((head != i) | (blk != j))
            def _():
                out_copy(i, j).wait_send()

    @pl.when(step == 0)
    def _():
        carry.wait_send()


def one_kernel(
    sizes,
    states, start, w_qkv, w_out, q_gain, k_gain, mod_table, step_index, coef_table, coef_index
):
    nh, nb = sizes
    n = nh * nb
    rows, width = start.shape
    depth, _, cols = w_qkv.shape
    own_cols = cols // nb
    out_cols = width // nb
    local_heads = own_cols // HD
    length = rows * n
    half16 = jnp.bfloat16
    vmem = pl.BlockSpec(memory_space=pltpu.VMEM)
    hbm = pl.BlockSpec(memory_space=pltpu.HBM)
    dma = pltpu.SemaphoreType.DMA
    return pl.pallas_call(
        functools.partial(whole_kernel, sizes),
        out_shape=jax.ShapeDtypeStruct(states.shape, jnp.float32),
        in_specs=[hbm] * 10,
        out_specs=vmem,
        scratch_shapes=[
            pltpu.VMEM(states.shape, jnp.float32),
            pltpu.VMEM(start.shape, jnp.float32),
            pltpu.VMEM((1, HD), jnp.float32),
            pltpu.VMEM((1, HD), jnp.float32),
            pltpu.SMEM(step_index.shape, jnp.int32),
            pltpu.SMEM(coef_table.shape, jnp.float32),
            pltpu.SMEM(coef_index.shape, jnp.int32),
            pltpu.VMEM((3, depth, cols), half16),
            pltpu.VMEM(mod_table.shape, jnp.float32),
            pltpu.VMEM((nb, rows, depth), half16),
            pltpu.VMEM((n, rows, depth), half16),
            pltpu.VMEM((nh, nb, nb * rows * 3 * own_cols // 128, 128), half16),
            pltpu.VMEM((nh, nb, nb * rows * 3 * own_cols // 128, 128), half16),
            pltpu.VMEM((nh, nb * rows, 3 * own_cols), jnp.float32),
            pltpu.VMEM((nh // 2, nb, 2 * nb * rows * own_cols // 128, 128), half16),
            pltpu.VMEM((nb, own_cols, out_cols), half16),
            pltpu.VMEM((n, rows, out_cols), half16),
            pltpu.VMEM((n, rows, out_cols), half16),
            pltpu.VMEM((rows, width), half16),
            pltpu.VMEM((rows, width), half16),
            pltpu.VMEM((local_heads, length, HD), half16),
            pltpu.VMEM((local_heads, length, HD), half16),
            pltpu.VMEM((local_heads, length, HD), half16),
            dma((10,)),
            dma((nb,)), dma((nb,)),
            dma((2 * nh,)), dma((nh,)),
            dma((n,)), dma((n,)),
            dma((nb * nh // 2,)), dma((nb * nh // 2,)),
            dma((nb,)), dma((nb,)),
            dma((nb,)), dma((nb,)),
            dma((n,)), dma((n,)),
            dma((1,)), dma((1,)),
        ],
        compiler_params=pltpu.CompilerParams(
            collective_id=0, has_side_effects=True, vmem_limit_bytes=56 * 1024 * 1024
        ),
        name="picard_step",
    )(
        states, start, jnp.transpose(w_qkv, (1, 0, 2)), w_out,
        q_gain[None], k_gain[None], mod_table, step_index, coef_table, coef_index,
    )


def on_device(sizes, *arrays):
    step_count, nh, nb = sizes
    states, start, w_qkv, w_out = arrays[:4]
    rows, width = start.shape
    depth, _, cols = w_qkv.shape
    fits = (
        step_count == 2
        and states.shape[0] == 1
        and nh % 2 == 0
        and nh & (nh - 1) == 0
        and rows % 16 == 0
        and cols % (nb * HD) == 0
        and w_out.shape[0] == cols // nb
        and (cols // nb) % 32 == 0
        and depth * nb == width
        and depth % 128 == 0
    )
    if fits:
        return one_kernel((nh, nb), *arrays)
    return general_plan(*arrays)


def solution(mesh):
    in_specs = (
        P("step", ("head", "blk"), None),
        P(("head", "blk"), None),
        P("blk", None, "head"),
        P(("head", "blk"), None),
        P(),
        P(),
        P(),
        P("step"),
        P(),
        P("step"),
    )
    out_specs = P("step", ("head", "blk"), None)
    sizes = (mesh.shape["step"], mesh.shape["head"], mesh.shape["blk"])
    return jax.shard_map(
        functools.partial(on_device, sizes), mesh=mesh, in_specs=in_specs, out_specs=out_specs, check_vma=False
    )
```

```python
import functools

import jax
import jax.numpy as jnp
from jax import lax
from jax.experimental import pallas as pl
from jax.experimental.pallas import tpu as pltpu
from jax.sharding import PartitionSpec as P

HD = 64
MESH = pl.DeviceIdType.MESH


def carried_in(array, axis, join, neutral):
    place = lax.axis_index(axis)
    gathered = lax.all_gather(array.astype(jnp.bfloat16), axis)
    state = jnp.zeros_like(array) + jnp.asarray(neutral, array.dtype)

    def one(step, state):
        return join(state, lax.dynamic_index_in_dim(gathered, step, 0, False).astype(array.dtype))

    return lax.fori_loop(0, place, one, state)


def head_norm(values_in, gains):
    middle = jnp.mean(values_in, axis=-1, keepdims=True)
    spread = jnp.mean((values_in - middle) ** 2, axis=-1, keepdims=True)
    return (values_in - middle) * lax.rsqrt(spread + 1e-06) * gains


def general_plan(
    states, start, w_qkv, w_out, q_gain, k_gain, mod_table, step_index, coef_table, coef_index
):
    width = states.shape[2]
    table_size = mod_table.shape[0]
    slot_ids = jnp.arange(table_size, dtype=jnp.int32)[None, :]
    mod_picks = (step_index[:, None] == slot_ids).astype(jnp.float32)
    coef_picks = (coef_index[:, None] == slot_ids).astype(jnp.float32)
    modulation = jnp.dot(mod_picks, mod_table, precision=lax.Precision.HIGHEST).reshape(
        -1, 3, width
    )
    coefs = jnp.sum(coef_picks * coef_table[None, :], axis=1)
    middle = jnp.mean(states, axis=-1, keepdims=True)
    spread = jnp.mean((states - middle) ** 2, axis=-1, keepdims=True)
    normed = (
        (states - middle) * lax.rsqrt(spread + 1e-05) * (1.0 + modulation[:, 1][:, None, :])
        + modulation[:, 0][:, None, :]
    ).astype(jnp.bfloat16)
    weight_rows = lax.all_gather(w_qkv, "blk", axis=0, tiled=True)
    projected = jnp.einsum(
        "std,dce->stce",
        lax.all_gather(normed, "head", axis=1, tiled=True),
        weight_rows,
        preferred_element_type=jnp.float32,
    )
    step_count = projected.shape[0]
    row_count = projected.shape[1]
    local_heads = projected.shape[3] // HD
    queries = head_norm(
        projected[:, :, 0].reshape(step_count, row_count, local_heads, HD), q_gain
    ).astype(jnp.bfloat16)
    keys_here = head_norm(
        projected[:, :, 1].reshape(step_count, row_count, local_heads, HD), k_gain
    ).astype(jnp.bfloat16)
    values_here = (
        projected[:, :, 2].reshape(step_count, row_count, local_heads, HD).astype(jnp.bfloat16)
    )
    scale_factor = HD ** (-0.5)
    start_best = jnp.full((step_count, local_heads, row_count), -1e30, jnp.float32)
    start_totals = jnp.zeros((step_count, local_heads, row_count), jnp.float32)
    start_accum = jnp.zeros((step_count, local_heads, row_count, HD), jnp.float32)
    best = start_best
    totals = start_totals
    accum = start_accum
    key_piece = lax.all_gather(keys_here, "blk", axis=1, tiled=True)
    value_piece = lax.all_gather(values_here, "blk", axis=1, tiled=True)
    length = key_piece.shape[1]
    for offset in range(0, length, 512):
        stop = min(offset + 512, length)
        key_block = key_piece[:, offset:stop]
        value_block = value_piece[:, offset:stop]
        scores = (
            jnp.einsum("sqhd,skhd->shqk", queries, key_block, preferred_element_type=jnp.float32)
            * scale_factor
        )
        new_best = jnp.maximum(best, jnp.max(scores, axis=-1))
        factor = jnp.exp(best - new_best)
        weights = jnp.exp(scores - new_best[..., None])
        totals = totals * factor + jnp.sum(weights, axis=-1)
        accum = accum * factor[..., None] + jnp.einsum(
            "shqk,skhd->shqd",
            weights.astype(jnp.bfloat16),
            value_block,
            preferred_element_type=jnp.float32,
        )
        best = new_best
    best, totals, accum = (best, totals, accum)
    attn = jnp.transpose(accum / totals[..., None], (0, 2, 1, 3)).reshape(
        step_count, row_count, local_heads * HD
    )
    attn = attn.astype(jnp.bfloat16)
    group_terms = jnp.einsum(
        "srf,fe->sre",
        attn,
        lax.all_gather(w_out, "blk", axis=0, tiled=True),
        preferred_element_type=jnp.float32,
    )
    mixed = lax.psum_scatter(
        group_terms.astype(jnp.bfloat16), "head", scatter_dimension=1, tiled=True
    ).astype(jnp.float32)
    drift = modulation[:, 2][:, None, :] * mixed
    inclusive = jnp.cumsum(coefs[:, None, None] * drift, axis=0)
    own_total = inclusive[-1]
    earlier = carried_in(
        own_total, "step", lambda first, second: first + second, jnp.zeros_like(own_total)
    )
    return start[None] + (earlier[None] + inclusive)


def paired(place, turn):
    bit = 1
    while bit <= turn:
        if turn & bit:
            place = place + bit * (1 - 2 * ((place // bit) % 2))
        bit *= 2
    return place


def pack(values):
    rows, cols = values.shape
    tiles = [values[:, at : at + 128] for at in range(0, cols - 127, 128)]
    if cols % 128:
        rest = values[:, cols - 64 :]
        tiles.append(jnp.concatenate([rest[: rows // 2], rest[rows // 2 :]], axis=1))
    return tiles


def unpack(buffer, rows, cols):
    full = cols // 128
    parts = [buffer[t * rows : (t + 1) * rows] for t in range(full)]
    if cols % 128:
        rest = buffer[full * rows :]
        parts.append(jnp.concatenate([rest[:, :64], rest[:, 64:]], axis=0))
    return jnp.concatenate(parts, axis=1)


def whole_kernel(
    sizes,
    states_hbm, start_hbm, w_qkv_ref, w_out_ref, q_gain_hbm, k_gain_hbm, mod_ref,
    step_index_hbm, coef_table_hbm, coef_index_hbm,
    out_ref,
    states_ref, start_ref, q_gain_ref, k_gain_ref, step_index_ref, coef_table_ref, coef_index_ref,
    w_buf, mod_buf, norm_send, norm_got, part_send, part_got, part_own, attn_buf, wo_buf,
    out_send, out_got, carry_send, carry_got, q_buf, k_buf, v_buf,
    local_sem, norm_ss, norm_rs, relay_ss, relay_rs, part_ss, part_rs, attn_ss, attn_rs,
    wo_ss, wo_rs, fwd_ss, fwd_rs, out_ss, out_rs, carry_ss, carry_rs,
):
    nh, nb = sizes
    n = nh * nb
    rows, width = start_ref.shape
    depth = w_buf.shape[1]
    own_cols = w_buf.shape[2] // nb
    out_cols = width // nb
    quarter = own_cols // 4
    local_heads = own_cols // HD
    group_rows = nb * rows
    step = lax.axis_index("step")
    head = lax.axis_index("head")
    blk = lax.axis_index("blk")
    me = head * nb + blk

    fetches = [
        pltpu.make_async_copy(source, target, local_sem.at[3 + place])
        for place, (source, target) in enumerate(
            (
                (states_hbm, states_ref),
                (step_index_hbm, step_index_ref),
                (q_gain_hbm, q_gain_ref),
                (k_gain_hbm, k_gain_ref),
                (coef_index_hbm, coef_index_ref),
                (coef_table_hbm, coef_table_ref),
                (start_hbm, start_ref),
            )
        )
    ]
    for fetch in fetches[:2]:
        fetch.start()
    mod_copy = pltpu.make_async_copy(mod_ref, mod_buf, local_sem.at[0])
    mod_copy.start()
    for fetch in fetches[2:]:
        fetch.start()
    w_copy = pltpu.make_async_copy(w_qkv_ref, w_buf, local_sem.at[1])
    w_copy.start()
    wo_copy = pltpu.make_async_copy(
        w_out_ref.at[:, pl.ds(pl.multiple_of(blk * out_cols, 128), out_cols)],
        wo_buf.at[blk],
        local_sem.at[2],
    )
    wo_copy.start()

    barrier = pltpu.get_barrier_semaphore()
    for e in range(1, nb):
        pl.semaphore_signal(
            barrier, inc=1, device_id=(step, head, (blk + e) % nb), device_id_type=MESH
        )
    pl.semaphore_signal(barrier, inc=1, device_id=(1 - step, head, blk), device_id_type=MESH)

    @pl.when(head > 0)
    def _():
        pl.semaphore_signal(barrier, inc=1, device_id=(step, head - 1, blk), device_id_type=MESH)

    @pl.when(head < nh - 1)
    def _():
        pl.semaphore_signal(barrier, inc=1, device_id=(step, head + 1, blk), device_id_type=MESH)

    fetches[0].wait()
    current = states_ref[0]
    middle = jnp.mean(current, axis=-1, keepdims=True)
    spread = jnp.mean((current - middle) ** 2, axis=-1, keepdims=True)
    fetches[1].wait()
    mod_copy.wait()
    slot = step_index_ref[0]
    shift = mod_buf[pl.ds(slot, 1), 0:width]
    scale = mod_buf[pl.ds(slot, 1), width : 2 * width]
    normed = (
        (current - middle) * lax.rsqrt(spread + 1e-05) * (1.0 + scale) + shift
    ).astype(jnp.bfloat16)
    for c in range(nb):
        norm_send[c] = normed[:, c * depth : (c + 1) * depth]
    norm_got[me] = norm_send[blk]
    pl.semaphore_wait(barrier, nb + jnp.minimum(head, 1) + jnp.minimum(nh - 1 - head, 1))

    def norm_copy(e):
        there = (blk + e) % nb
        return pltpu.make_async_remote_copy(
            src_ref=norm_send.at[there],
            dst_ref=norm_got.at[me],
            send_sem=norm_ss.at[e],
            recv_sem=norm_rs.at[blk],
            device_id=(step, head, there),
            device_id_type=MESH,
        )

    def norm_arrival(e):
        source = (blk + e) % nb
        return pltpu.make_async_remote_copy(
            src_ref=norm_send.at[0],
            dst_ref=norm_got.at[head * nb + source],
            send_sem=norm_ss.at[0],
            recv_sem=norm_rs.at[source],
            device_id=(step, head, blk),
            device_id_type=MESH,
        )

    def relay(origin, way):
        place = norm_got.at[pl.ds(origin * nb, nb)]
        return pltpu.make_async_remote_copy(
            src_ref=place,
            dst_ref=place,
            send_sem=relay_ss.at[way * nh + origin],
            recv_sem=relay_rs.at[origin],
            device_id=(step, head + 1 - 2 * way, blk),
            device_id_type=MESH,
        )

    def upward(origin):
        @pl.when(head < nh - 1)
        def _():
            relay(origin, 0).start()

    def downward(origin):
        @pl.when(head > 0)
        def _():
            relay(origin, 1).start()

    for e in range(1, nb):
        norm_copy(e).start()

    def wo_rows(which, p):
        return pl.ds(pl.multiple_of((2 * which + p) * quarter, 16), quarter)

    def wo_send(p, e):
        there = (blk + e) % nb
        return pltpu.make_async_remote_copy(
            src_ref=w_out_ref.at[
                wo_rows(step, p), pl.ds(pl.multiple_of(there * out_cols, 128), out_cols)
            ],
            dst_ref=wo_buf.at[blk, wo_rows(step, p)],
            send_sem=wo_ss.at[p * nb + e],
            recv_sem=wo_rs.at[p * nb + blk],
            device_id=(step, head, there),
            device_id_type=MESH,
        )

    def wo_part(source, which, p, sems, rsems, e):
        place = wo_buf.at[source, wo_rows(which, p)]
        return pltpu.make_async_remote_copy(
            src_ref=place,
            dst_ref=place,
            send_sem=sems.at[p * nb + e],
            recv_sem=rsems.at[p * nb + source],
            device_id=(1 - step, head, blk),
            device_id_type=MESH,
        )

    def wo_pass(p):
        for e in range(1, nb):
            source = (blk + e) % nb
            wo_part(source, step, p, wo_ss, wo_rs, 0).wait_recv()
            wo_part(source, step, p, fwd_ss, fwd_rs, e).start()

    for e in range(1, nb):
        wo_send(0, e).start()

    def part_copy(i, e):
        there = (blk + e) % nb
        return pltpu.make_async_remote_copy(
            src_ref=part_send.at[i, there],
            dst_ref=part_got.at[i, blk],
            send_sem=part_ss.at[i * nb + e],
            recv_sem=part_rs.at[i * nb + blk],
            device_id=(step, head, there),
            device_id_type=MESH,
        )

    def part_arrival(i, e):
        source = (blk + e) % nb
        return pltpu.make_async_remote_copy(
            src_ref=part_send.at[i, 0],
            dst_ref=part_got.at[i, source],
            send_sem=part_ss.at[0],
            recv_sem=part_rs.at[i * nb + source],
            device_id=(step, head, blk),
            device_id_type=MESH,
        )

    for e in range(1, nb):
        norm_arrival(e).wait_recv()
    upward(head)
    downward(head)
    w_copy.wait()

    def project(i):
        tokens = norm_got[pl.ds(i * nb, nb)].reshape(group_rows, depth)
        terms = [
            jnp.dot(tokens, w_buf[c], preferred_element_type=jnp.float32) for c in range(3)
        ]
        for c in range(nb):
            share = jnp.concatenate(
                [term[:, c * own_cols : (c + 1) * own_cols] for term in terms], axis=1
            )

            @pl.when(blk == c)
            def _():
                part_own[i] = share

            @pl.when(blk != c)
            def _():
                packed = pack(share.astype(jnp.bfloat16))
                for t, tile in enumerate(packed):
                    part_send[i, c, t * group_rows : t * group_rows + tile.shape[0]] = tile

        for e in range(1, nb):
            part_copy(i, e).start()

    project(head)

    def further(d, carried):
        low, high = head - d, head + d

        @pl.when(low >= 0)
        def _():
            relay(low, 0).wait_recv()
            upward(low)

        @pl.when(high < nh)
        def _():
            relay(high, 0).wait_recv()
            downward(high)

        @pl.when(low >= 0)
        def _():
            project(low)

        @pl.when(high < nh)
        def _():
            project(high)

        return carried

    lax.fori_loop(1, nh, further, 0)

    for e in range(1, nb):
        wo_send(1, e).start()
    wo_pass(0)

    def head_parts(values, gains):
        center = jnp.mean(values, axis=-1, keepdims=True)
        width_sq = jnp.mean((values - center) ** 2, axis=-1, keepdims=True)
        return (values - center) * lax.rsqrt(width_sq + 1e-06) * gains

    fetches[2].wait()
    fetches[3].wait()

    def finish(i, carried):
        total = part_own[i]
        for e in range(1, nb):
            part_arrival(i, e).wait_recv()
            total = total + unpack(
                part_got.at[i, (blk + e) % nb], group_rows, 3 * own_cols
            ).astype(jnp.float32)
        upper = i // (nh // 2)
        place = (1 - upper) * 2 * i + upper * (2 * (nh - 1 - i) + 1)
        here = pl.ds(pl.multiple_of(place * group_rows, group_rows), group_rows)
        for g in range(local_heads):
            at = g * HD
            q_buf[g, here] = head_parts(total[:, at : at + HD], q_gain_ref[...]).astype(
                jnp.bfloat16
            )
            at += own_cols
            k_buf[g, here] = head_parts(total[:, at : at + HD], k_gain_ref[...]).astype(
                jnp.bfloat16
            )
            at += own_cols
            v_buf[g, here] = total[:, at : at + HD].astype(jnp.bfloat16)
        return carried

    for i in range(nh):
        finish(paired(head, i), 0)

    def attn_copy(s, e):
        there = (blk + e) % nb
        return pltpu.make_async_remote_copy(
            src_ref=attn_buf.at[s, blk],
            dst_ref=attn_buf.at[s, blk],
            send_sem=attn_ss.at[s * nb + e],
            recv_sem=attn_rs.at[s * nb + blk],
            device_id=(step, head, there),
            device_id_type=MESH,
        )

    def attn_arrival(s, e):
        source = (blk + e) % nb
        return pltpu.make_async_remote_copy(
            src_ref=attn_buf.at[s, blk],
            dst_ref=attn_buf.at[s, source],
            send_sem=attn_ss.at[0],
            recv_sem=attn_rs.at[s * nb + source],
            device_id=(step, head, blk),
            device_id_type=MESH,
        )

    pair_rows = 2 * group_rows
    pairs = range(nh // 2)
    for s in pairs:
        here = slice(s * pair_rows, (s + 1) * pair_rows)
        mixed = []
        for g in range(local_heads):
            scores = lax.dot_general(
                q_buf[g, here],
                k_buf[g],
                (((1,), (1,)), ((), ())),
                preferred_element_type=jnp.float32,
            ) * (HD ** (-0.5))
            weights = jnp.exp(scores - jnp.max(scores, axis=-1, keepdims=True))
            totals = jnp.sum(weights, axis=-1, keepdims=True)
            value = jnp.dot(
                weights.astype(jnp.bfloat16), v_buf[g], preferred_element_type=jnp.float32
            )
            mixed.append((value / totals).astype(jnp.bfloat16))
        for t, tile in enumerate(pack(jnp.concatenate(mixed, axis=1))):
            attn_buf[s, blk, t * pair_rows : t * pair_rows + tile.shape[0]] = tile
        for e in range(1, nb):
            attn_copy(s, e).start()
        if s == 0:
            wo_pass(1)

    wo_copy.wait()
    for e in range(1, nb):
        source = (blk + e) % nb
        for p in range(2):
            wo_part(source, 1 - step, p, fwd_ss, fwd_rs, 0).wait_recv()

    def out_place(i):
        return 2 * i if i < nh // 2 else 2 * (nh - 1 - i) + 1

    def out_copy(i, j):
        return pltpu.make_async_remote_copy(
            src_ref=out_send.at[out_place(i) * nb + j],
            dst_ref=out_got.at[me],
            send_sem=out_ss.at[i * nb + j],
            recv_sem=out_rs.at[me],
            device_id=(step, i, j),
            device_id_type=MESH,
        )

    def out_arrival(source):
        return pltpu.make_async_remote_copy(
            src_ref=out_send.at[0],
            dst_ref=out_got.at[source],
            send_sem=out_ss.at[0],
            recv_sem=out_rs.at[source],
            device_id=(step, head, blk),
            device_id_type=MESH,
        )

    for s in pairs:
        drift = jnp.dot(
            unpack(attn_buf[s, blk], pair_rows, own_cols),
            wo_buf[blk],
            preferred_element_type=jnp.float32,
        )
        for e in range(1, nb):
            source = (blk + e) % nb
            attn_arrival(s, e).wait_recv()
            drift = drift + jnp.dot(
                unpack(attn_buf[s, source], pair_rows, own_cols),
                wo_buf[source],
                preferred_element_type=jnp.float32,
            )
        out_send[2 * s * nb : 2 * (s + 1) * nb] = drift.astype(jnp.bfloat16).reshape(
            2 * nb, rows, out_cols
        )
        for i in (s, nh - 1 - s):
            for j in range(nb):
                @pl.when((head != i) | (blk != j))
                def _():
                    out_copy(i, j).start()
    upper = head // (nh // 2)
    own_place = (1 - upper) * 2 * head + upper * (2 * (nh - 1 - head) + 1)
    out_got[me] = out_send[own_place * nb + blk]

    for fetch in fetches[4:]:
        fetch.wait()
    coef = coef_table_ref[coef_index_ref[0]]
    for d in range(1, n):
        out_arrival((me + d) % n).wait_recv()

    moved = []
    for c in range(nb):
        total = out_got[c].astype(jnp.float32)
        for h in range(1, nh):
            total = total + out_got[h * nb + c].astype(jnp.float32)
        gate = mod_buf[
            pl.ds(slot, 1), 2 * width + c * out_cols : 2 * width + (c + 1) * out_cols
        ]
        moved.append(coef * (gate * total))

    carry = pltpu.make_async_remote_copy(
        src_ref=carry_send,
        dst_ref=carry_got,
        send_sem=carry_ss.at[0],
        recv_sem=carry_rs.at[0],
        device_id=(1 - step, head, blk),
        device_id_type=MESH,
    )

    @pl.when(step == 0)
    def _():
        for c in range(nb):
            carry_send[:, c * out_cols : (c + 1) * out_cols] = moved[c].astype(jnp.bfloat16)
        carry.start()
        for c in range(nb):
            cols = slice(c * out_cols, (c + 1) * out_cols)
            out_ref[0, :, cols] = start_ref[:, cols] + moved[c]

    @pl.when(step == 1)
    def _():
        carry.wait_recv()
        for c in range(nb):
            cols = slice(c * out_cols, (c + 1) * out_cols)
            out_ref[0, :, cols] = start_ref[:, cols] + (
                carry_got[:, cols].astype(jnp.float32) + moved[c]
            )

    for i in range(nh):
        @pl.when((i <= head) & (head < nh - 1))
        def _():
            relay(i, 0).wait_send()

        @pl.when((i >= head) & (head > 0))
        def _():
            relay(i, 1).wait_send()

    for e in range(1, nb):
        norm_copy(e).wait_send()
        for p in range(2):
            wo_send(p, e).wait_send()
            wo_part((blk + e) % nb, step, p, fwd_ss, fwd_rs, e).wait_send()
        for s in pairs:
            attn_copy(s, e).wait_send()
        for i in range(nh):
            part_copy(i, e).wait_send()
    for i in range(nh):
        for j in range(nb):
            @pl.when((head != i) | (blk != j))
            def _():
                out_copy(i, j).wait_send()

    @pl.when(step == 0)
    def _():
        carry.wait_send()


def one_kernel(
    sizes,
    states, start, w_qkv, w_out, q_gain, k_gain, mod_table, step_index, coef_table, coef_index
):
    nh, nb = sizes
    n = nh * nb
    rows, width = start.shape
    depth, _, cols = w_qkv.shape
    own_cols = cols // nb
    out_cols = width // nb
    local_heads = own_cols // HD
    length = rows * n
    half16 = jnp.bfloat16
    vmem = pl.BlockSpec(memory_space=pltpu.VMEM)
    hbm = pl.BlockSpec(memory_space=pltpu.HBM)
    dma = pltpu.SemaphoreType.DMA
    return pl.pallas_call(
        functools.partial(whole_kernel, sizes),
        out_shape=jax.ShapeDtypeStruct(states.shape, jnp.float32),
        in_specs=[hbm] * 10,
        out_specs=vmem,
        scratch_shapes=[
            pltpu.VMEM(states.shape, jnp.float32),
            pltpu.VMEM(start.shape, jnp.float32),
            pltpu.VMEM((1, HD), jnp.float32),
            pltpu.VMEM((1, HD), jnp.float32),
            pltpu.SMEM(step_index.shape, jnp.int32),
            pltpu.SMEM(coef_table.shape, jnp.float32),
            pltpu.SMEM(coef_index.shape, jnp.int32),
            pltpu.VMEM((3, depth, cols), half16),
            pltpu.VMEM(mod_table.shape, jnp.float32),
            pltpu.VMEM((nb, rows, depth), half16),
            pltpu.VMEM((n, rows, depth), half16),
            pltpu.VMEM((nh, nb, nb * rows * 3 * own_cols // 128, 128), half16),
            pltpu.VMEM((nh, nb, nb * rows * 3 * own_cols // 128, 128), half16),
            pltpu.VMEM((nh, nb * rows, 3 * own_cols), jnp.float32),
            pltpu.VMEM((nh // 2, nb, 2 * nb * rows * own_cols // 128, 128), half16),
            pltpu.VMEM((nb, own_cols, out_cols), half16),
            pltpu.VMEM((n, rows, out_cols), half16),
            pltpu.VMEM((n, rows, out_cols), half16),
            pltpu.VMEM((rows, width), half16),
            pltpu.VMEM((rows, width), half16),
            pltpu.VMEM((local_heads, length, HD), half16),
            pltpu.VMEM((local_heads, length, HD), half16),
            pltpu.VMEM((local_heads, length, HD), half16),
            dma((10,)),
            dma((nb,)), dma((nb,)),
            dma((2 * nh,)), dma((nh,)),
            dma((n,)), dma((n,)),
            dma((nb * nh // 2,)), dma((nb * nh // 2,)),
            dma((2 * nb,)), dma((2 * nb,)),
            dma((2 * nb,)), dma((2 * nb,)),
            dma((n,)), dma((n,)),
            dma((1,)), dma((1,)),
        ],
        compiler_params=pltpu.CompilerParams(
            collective_id=0, has_side_effects=True, vmem_limit_bytes=56 * 1024 * 1024
        ),
        name="picard_step",
    )(
        states, start, jnp.transpose(w_qkv, (1, 0, 2)), w_out,
        q_gain[None], k_gain[None], mod_table, step_index, coef_table, coef_index,
    )


def on_device(sizes, *arrays):
    step_count, nh, nb = sizes
    states, start, w_qkv, w_out = arrays[:4]
    rows, width = start.shape
    depth, _, cols = w_qkv.shape
    fits = (
        step_count == 2
        and states.shape[0] == 1
        and nh % 2 == 0
        and nh & (nh - 1) == 0
        and rows % 16 == 0
        and cols % (nb * HD) == 0
        and w_out.shape[0] == cols // nb
        and (cols // nb) % 64 == 0
        and depth * nb == width
        and depth % 128 == 0
    )
    if fits:
        return one_kernel((nh, nb), *arrays)
    return general_plan(*arrays)


def solution(mesh):
    in_specs = (
        P("step", ("head", "blk"), None),
        P(("head", "blk"), None),
        P("blk", None, "head"),
        P(("head", "blk"), None),
        P(),
        P(),
        P(),
        P("step"),
        P(),
        P("step"),
    )
    out_specs = P("step", ("head", "blk"), None)
    sizes = (mesh.shape["step"], mesh.shape["head"], mesh.shape["blk"])
    return jax.shard_map(
        functools.partial(on_device, sizes), mesh=mesh, in_specs=in_specs, out_specs=out_specs, check_vma=False
    )
```

```python
import functools

import jax
import jax.numpy as jnp
from jax import lax
from jax.experimental import pallas as pl
from jax.experimental.pallas import tpu as pltpu
from jax.sharding import PartitionSpec as P

HD = 64
MESH = pl.DeviceIdType.MESH


def carried_in(array, axis, join, neutral):
    place = lax.axis_index(axis)
    gathered = lax.all_gather(array.astype(jnp.bfloat16), axis)
    state = jnp.zeros_like(array) + jnp.asarray(neutral, array.dtype)

    def one(step, state):
        return join(state, lax.dynamic_index_in_dim(gathered, step, 0, False).astype(array.dtype))

    return lax.fori_loop(0, place, one, state)


def head_norm(values_in, gains):
    middle = jnp.mean(values_in, axis=-1, keepdims=True)
    spread = jnp.mean((values_in - middle) ** 2, axis=-1, keepdims=True)
    return (values_in - middle) * lax.rsqrt(spread + 1e-06) * gains


def general_plan(
    states, start, w_qkv, w_out, q_gain, k_gain, mod_table, step_index, coef_table, coef_index
):
    width = states.shape[2]
    table_size = mod_table.shape[0]
    slot_ids = jnp.arange(table_size, dtype=jnp.int32)[None, :]
    mod_picks = (step_index[:, None] == slot_ids).astype(jnp.float32)
    coef_picks = (coef_index[:, None] == slot_ids).astype(jnp.float32)
    modulation = jnp.dot(mod_picks, mod_table, precision=lax.Precision.HIGHEST).reshape(
        -1, 3, width
    )
    coefs = jnp.sum(coef_picks * coef_table[None, :], axis=1)
    middle = jnp.mean(states, axis=-1, keepdims=True)
    spread = jnp.mean((states - middle) ** 2, axis=-1, keepdims=True)
    normed = (
        (states - middle) * lax.rsqrt(spread + 1e-05) * (1.0 + modulation[:, 1][:, None, :])
        + modulation[:, 0][:, None, :]
    ).astype(jnp.bfloat16)
    weight_rows = lax.all_gather(w_qkv, "blk", axis=0, tiled=True)
    projected = jnp.einsum(
        "std,dce->stce",
        lax.all_gather(normed, "head", axis=1, tiled=True),
        weight_rows,
        preferred_element_type=jnp.float32,
    )
    step_count = projected.shape[0]
    row_count = projected.shape[1]
    local_heads = projected.shape[3] // HD
    queries = head_norm(
        projected[:, :, 0].reshape(step_count, row_count, local_heads, HD), q_gain
    ).astype(jnp.bfloat16)
    keys_here = head_norm(
        projected[:, :, 1].reshape(step_count, row_count, local_heads, HD), k_gain
    ).astype(jnp.bfloat16)
    values_here = (
        projected[:, :, 2].reshape(step_count, row_count, local_heads, HD).astype(jnp.bfloat16)
    )
    scale_factor = HD ** (-0.5)
    start_best = jnp.full((step_count, local_heads, row_count), -1e30, jnp.float32)
    start_totals = jnp.zeros((step_count, local_heads, row_count), jnp.float32)
    start_accum = jnp.zeros((step_count, local_heads, row_count, HD), jnp.float32)
    best = start_best
    totals = start_totals
    accum = start_accum
    key_piece = lax.all_gather(keys_here, "blk", axis=1, tiled=True)
    value_piece = lax.all_gather(values_here, "blk", axis=1, tiled=True)
    length = key_piece.shape[1]
    for offset in range(0, length, 512):
        stop = min(offset + 512, length)
        key_block = key_piece[:, offset:stop]
        value_block = value_piece[:, offset:stop]
        scores = (
            jnp.einsum("sqhd,skhd->shqk", queries, key_block, preferred_element_type=jnp.float32)
            * scale_factor
        )
        new_best = jnp.maximum(best, jnp.max(scores, axis=-1))
        factor = jnp.exp(best - new_best)
        weights = jnp.exp(scores - new_best[..., None])
        totals = totals * factor + jnp.sum(weights, axis=-1)
        accum = accum * factor[..., None] + jnp.einsum(
            "shqk,skhd->shqd",
            weights.astype(jnp.bfloat16),
            value_block,
            preferred_element_type=jnp.float32,
        )
        best = new_best
    best, totals, accum = (best, totals, accum)
    attn = jnp.transpose(accum / totals[..., None], (0, 2, 1, 3)).reshape(
        step_count, row_count, local_heads * HD
    )
    attn = attn.astype(jnp.bfloat16)
    group_terms = jnp.einsum(
        "srf,fe->sre",
        attn,
        lax.all_gather(w_out, "blk", axis=0, tiled=True),
        preferred_element_type=jnp.float32,
    )
    mixed = lax.psum_scatter(
        group_terms.astype(jnp.bfloat16), "head", scatter_dimension=1, tiled=True
    ).astype(jnp.float32)
    drift = modulation[:, 2][:, None, :] * mixed
    inclusive = jnp.cumsum(coefs[:, None, None] * drift, axis=0)
    own_total = inclusive[-1]
    earlier = carried_in(
        own_total, "step", lambda first, second: first + second, jnp.zeros_like(own_total)
    )
    return start[None] + (earlier[None] + inclusive)


def paired(place, turn):
    bit = 1
    while bit <= turn:
        if turn & bit:
            place = place + bit * (1 - 2 * ((place // bit) % 2))
        bit *= 2
    return place


def pack(values):
    rows, cols = values.shape
    tiles = [values[:, at : at + 128] for at in range(0, cols - 127, 128)]
    if cols % 128:
        rest = values[:, cols - 64 :]
        tiles.append(jnp.concatenate([rest[: rows // 2], rest[rows // 2 :]], axis=1))
    return tiles


def unpack(buffer, rows, cols):
    full = cols // 128
    parts = [buffer[t * rows : (t + 1) * rows] for t in range(full)]
    if cols % 128:
        rest = buffer[full * rows :]
        parts.append(jnp.concatenate([rest[:, :64], rest[:, 64:]], axis=0))
    return jnp.concatenate(parts, axis=1)


def whole_kernel(
    sizes,
    states_hbm, start_hbm, w_qkv_ref, w_out_ref, q_gain_hbm, k_gain_hbm, mod_ref,
    step_index_hbm, coef_table_hbm, coef_index_hbm,
    out_ref,
    states_ref, start_ref, q_gain_ref, k_gain_ref, step_index_ref, coef_table_ref, coef_index_ref,
    w_buf, mod_buf, norm_send, norm_got, one_send, one_got, two_send, two_got, part_own, attn_buf, wo_buf,
    out_send, out_got, out_rest, carry_send, carry_got, q_buf, k_buf, v_buf,
    local_sem, norm_ss, norm_rs, relay_ss, relay_rs, one_ss, one_rs, two_ss, two_rs, attn_ss, attn_rs,
    wo_ss, wo_rs, fwd_ss, fwd_rs, out_ss, out_rs, carry_ss, carry_rs,
):
    nh, nb = sizes
    n = nh * nb
    rows, width = start_ref.shape
    depth = w_buf.shape[1]
    own_cols = w_buf.shape[2] // nb
    out_cols = width // nb
    quarter = own_cols // 4
    local_heads = own_cols // HD
    group_rows = nb * rows
    step = lax.axis_index("step")
    head = lax.axis_index("head")
    blk = lax.axis_index("blk")
    me = head * nb + blk

    fetches = [
        pltpu.make_async_copy(source, target, local_sem.at[3 + place])
        for place, (source, target) in enumerate(
            (
                (states_hbm, states_ref),
                (step_index_hbm, step_index_ref),
                (q_gain_hbm, q_gain_ref),
                (k_gain_hbm, k_gain_ref),
                (coef_index_hbm, coef_index_ref),
                (coef_table_hbm, coef_table_ref),
                (start_hbm, start_ref),
            )
        )
    ]
    for fetch in fetches[:2]:
        fetch.start()
    mod_copy = pltpu.make_async_copy(mod_ref, mod_buf, local_sem.at[0])
    mod_copy.start()
    for fetch in fetches[2:]:
        fetch.start()
    w_copy = pltpu.make_async_copy(w_qkv_ref, w_buf, local_sem.at[1])
    wo_copy = pltpu.make_async_copy(
        w_out_ref.at[:, pl.ds(pl.multiple_of(blk * out_cols, 128), out_cols)],
        wo_buf.at[blk],
        local_sem.at[2],
    )
    wo_copy.start()

    barrier = pltpu.get_barrier_semaphore()
    for e in range(1, nb):
        pl.semaphore_signal(
            barrier, inc=1, device_id=(step, head, (blk + e) % nb), device_id_type=MESH
        )
    pl.semaphore_signal(barrier, inc=1, device_id=(1 - step, head, blk), device_id_type=MESH)

    @pl.when(head > 0)
    def _():
        pl.semaphore_signal(barrier, inc=1, device_id=(step, head - 1, blk), device_id_type=MESH)

    @pl.when(head < nh - 1)
    def _():
        pl.semaphore_signal(barrier, inc=1, device_id=(step, head + 1, blk), device_id_type=MESH)

    fetches[0].wait()
    current = states_ref[0]
    middle = jnp.mean(current, axis=-1, keepdims=True)
    spread = jnp.mean((current - middle) ** 2, axis=-1, keepdims=True)
    fetches[1].wait()
    mod_copy.wait()
    w_copy.start()
    slot = step_index_ref[0]
    shift = mod_buf[pl.ds(slot, 1), 0:width]
    scale = mod_buf[pl.ds(slot, 1), width : 2 * width]
    normed = (
        (current - middle) * lax.rsqrt(spread + 1e-05) * (1.0 + scale) + shift
    ).astype(jnp.bfloat16)
    for c in range(nb):
        norm_send[c] = normed[:, c * depth : (c + 1) * depth]
    norm_got[me] = norm_send[blk]
    pl.semaphore_wait(barrier, nb + jnp.minimum(head, 1) + jnp.minimum(nh - 1 - head, 1))

    def norm_copy(e):
        there = (blk + e) % nb
        return pltpu.make_async_remote_copy(
            src_ref=norm_send.at[there],
            dst_ref=norm_got.at[me],
            send_sem=norm_ss.at[e],
            recv_sem=norm_rs.at[blk],
            device_id=(step, head, there),
            device_id_type=MESH,
        )

    def norm_arrival(e):
        source = (blk + e) % nb
        return pltpu.make_async_remote_copy(
            src_ref=norm_send.at[0],
            dst_ref=norm_got.at[head * nb + source],
            send_sem=norm_ss.at[0],
            recv_sem=norm_rs.at[source],
            device_id=(step, head, blk),
            device_id_type=MESH,
        )

    def relay(origin, way):
        place = norm_got.at[pl.ds(origin * nb, nb)]
        return pltpu.make_async_remote_copy(
            src_ref=place,
            dst_ref=place,
            send_sem=relay_ss.at[way * nh + origin],
            recv_sem=relay_rs.at[origin],
            device_id=(step, head + 1 - 2 * way, blk),
            device_id_type=MESH,
        )

    def upward(origin):
        @pl.when(head < nh - 1)
        def _():
            relay(origin, 0).start()

    def downward(origin):
        @pl.when(head > 0)
        def _():
            relay(origin, 1).start()

    for e in range(1, nb):
        norm_copy(e).start()

    def wo_rows(which, p):
        return pl.ds(pl.multiple_of((2 * which + p) * quarter, 16), quarter)

    def wo_send(p, e):
        there = (blk + e) % nb
        return pltpu.make_async_remote_copy(
            src_ref=w_out_ref.at[
                wo_rows(step, p), pl.ds(pl.multiple_of(there * out_cols, 128), out_cols)
            ],
            dst_ref=wo_buf.at[blk, wo_rows(step, p)],
            send_sem=wo_ss.at[p * nb + e],
            recv_sem=wo_rs.at[p * nb + blk],
            device_id=(step, head, there),
            device_id_type=MESH,
        )

    def wo_part(source, which, p, sems, rsems, e):
        place = wo_buf.at[source, wo_rows(which, p)]
        return pltpu.make_async_remote_copy(
            src_ref=place,
            dst_ref=place,
            send_sem=sems.at[p * nb + e],
            recv_sem=rsems.at[p * nb + source],
            device_id=(1 - step, head, blk),
            device_id_type=MESH,
        )

    def wo_pass(p):
        for e in range(1, nb):
            source = (blk + e) % nb
            wo_part(source, step, p, wo_ss, wo_rs, 0).wait_recv()
            wo_part(source, step, p, fwd_ss, fwd_rs, e).start()

    for e in range(1, nb):
        wo_send(0, e).start()

    by_x = blk + 1 - 2 * (blk % 2)
    by_y = blk + 2 - 4 * (blk // 2)
    across = nb - 1 - blk
    split = group_rows // 2
    mates = (by_x, by_y)
    span = (slice(0, split), slice(split, group_rows))

    def stage_one(i, way):
        return pltpu.make_async_remote_copy(
            src_ref=one_send.at[i, way],
            dst_ref=one_got.at[i, way],
            send_sem=one_ss.at[2 * i + way],
            recv_sem=one_rs.at[2 * i + way],
            device_id=(step, head, mates[way]),
            device_id_type=MESH,
        )

    def stage_two(i, way):
        return pltpu.make_async_remote_copy(
            src_ref=two_send.at[i, way],
            dst_ref=two_got.at[i, way],
            send_sem=two_ss.at[2 * i + way],
            recv_sem=two_rs.at[2 * i + way],
            device_id=(step, head, mates[1 - way]),
            device_id_type=MESH,
        )

    def lay(buffer, place, values):
        count = values.shape[0]
        for t, tile in enumerate(pack(values.astype(jnp.bfloat16))):
            buffer[*place, t * count : t * count + tile.shape[0]] = tile

    def lifted(buffer):
        return unpack(buffer, split, 3 * own_cols).astype(jnp.float32)

    for e in range(1, nb):
        norm_arrival(e).wait_recv()
    upward(head)
    downward(head)
    w_copy.wait()

    def project(i):
        tokens = norm_got[pl.ds(i * nb, nb)].reshape(group_rows, depth)
        terms = [
            jnp.dot(tokens, w_buf[c], preferred_element_type=jnp.float32) for c in range(3)
        ]
        for c in range(nb):
            part_own[i, c] = jnp.concatenate(
                [term[:, c * own_cols : (c + 1) * own_cols] for term in terms], axis=1
            )
        for way in range(2):
            lay(one_send, (i, way, 0), part_own[i, mates[way], span[way]])
            lay(one_send, (i, way, 1), part_own[i, across, span[way]])
            stage_one(i, way).start()

    def second(i):
        for way in range(2):
            stage_one(i, way).wait_recv()
            lay(
                two_send,
                (i, way),
                part_own[i, mates[1 - way], span[way]] + lifted(one_got.at[i, way, 1]),
            )
            stage_two(i, way).start()

    project(head)

    def further(d, carried):
        low, high = head - d, head + d

        @pl.when(low >= 0)
        def _():
            relay(low, 0).wait_recv()
            upward(low)

        @pl.when(high < nh)
        def _():
            relay(high, 0).wait_recv()
            downward(high)

        @pl.when(d == 1)
        def _():
            second(head)

        @pl.when((d > 1) & (low + 1 >= 0))
        def _():
            second(low + 1)

        @pl.when((d > 1) & (high - 1 < nh))
        def _():
            second(high - 1)

        @pl.when(low >= 0)
        def _():
            project(low)

        @pl.when(high < nh)
        def _():
            project(high)

        return carried

    lax.fori_loop(1, nh, further, 0)

    @pl.when(head == nh - 1)
    def _():
        second(0)

    @pl.when(head == 0)
    def _():
        second(nh - 1)

    for e in range(1, nb):
        wo_send(1, e).start()
    wo_pass(0)

    def head_parts(values, gains):
        center = jnp.mean(values, axis=-1, keepdims=True)
        width_sq = jnp.mean((values - center) ** 2, axis=-1, keepdims=True)
        return (values - center) * lax.rsqrt(width_sq + 1e-06) * gains

    fetches[2].wait()
    fetches[3].wait()

    def finish(i, carried):
        both = []
        for way in range(2):
            stage_two(i, way).wait_recv()
            both.append(
                part_own[i, blk, span[way]]
                + lifted(one_got.at[i, way, 0])
                + lifted(two_got.at[i, way])
            )
        total = jnp.concatenate(both, axis=0)
        upper = i // (nh // 2)
        place = (1 - upper) * 2 * i + upper * (2 * (nh - 1 - i) + 1)
        here = pl.ds(pl.multiple_of(place * group_rows, group_rows), group_rows)
        for g in range(local_heads):
            at = g * HD
            q_buf[g, here] = head_parts(total[:, at : at + HD], q_gain_ref[...]).astype(
                jnp.bfloat16
            )
            at += own_cols
            k_buf[g, here] = head_parts(total[:, at : at + HD], k_gain_ref[...]).astype(
                jnp.bfloat16
            )
            at += own_cols
            v_buf[g, here] = total[:, at : at + HD].astype(jnp.bfloat16)
        return carried

    for i in range(nh):
        finish(paired(head, i), 0)

    def attn_copy(s, e):
        there = (blk + e) % nb
        return pltpu.make_async_remote_copy(
            src_ref=attn_buf.at[s, blk],
            dst_ref=attn_buf.at[s, blk],
            send_sem=attn_ss.at[s * nb + e],
            recv_sem=attn_rs.at[s * nb + blk],
            device_id=(step, head, there),
            device_id_type=MESH,
        )

    def attn_arrival(s, e):
        source = (blk + e) % nb
        return pltpu.make_async_remote_copy(
            src_ref=attn_buf.at[s, blk],
            dst_ref=attn_buf.at[s, source],
            send_sem=attn_ss.at[0],
            recv_sem=attn_rs.at[s * nb + source],
            device_id=(step, head, blk),
            device_id_type=MESH,
        )

    pair_rows = 2 * group_rows
    pairs = range(nh // 2)
    for s in pairs:
        here = slice(s * pair_rows, (s + 1) * pair_rows)
        mixed = []
        for g in range(local_heads):
            scores = lax.dot_general(
                q_buf[g, here],
                k_buf[g],
                (((1,), (1,)), ((), ())),
                preferred_element_type=jnp.float32,
            ) * (HD ** (-0.5))
            weights = jnp.exp(scores - jnp.max(scores, axis=-1, keepdims=True))
            totals = jnp.sum(weights, axis=-1, keepdims=True)
            value = jnp.dot(
                weights.astype(jnp.bfloat16), v_buf[g], preferred_element_type=jnp.float32
            )
            mixed.append((value / totals).astype(jnp.bfloat16))
        for t, tile in enumerate(pack(jnp.concatenate(mixed, axis=1))):
            attn_buf[s, blk, t * pair_rows : t * pair_rows + tile.shape[0]] = tile
        for e in range(1, nb):
            attn_copy(s, e).start()
        if s == 0:
            wo_pass(1)

    wo_copy.wait()
    for e in range(1, nb):
        source = (blk + e) % nb
        for p in range(2):
            wo_part(source, 1 - step, p, fwd_ss, fwd_rs, 0).wait_recv()

    def out_place(i):
        return 2 * i if i < nh // 2 else 2 * (nh - 1 - i) + 1

    def out_copy(i, j):
        return pltpu.make_async_remote_copy(
            src_ref=out_send.at[out_place(i) * nb + j],
            dst_ref=out_got.at[me],
            send_sem=out_ss.at[i * nb + j],
            recv_sem=out_rs.at[me],
            device_id=(step, i, j),
            device_id_type=MESH,
        )

    def out_arrival(source):
        return pltpu.make_async_remote_copy(
            src_ref=out_send.at[0],
            dst_ref=out_got.at[source],
            send_sem=out_ss.at[0],
            recv_sem=out_rs.at[source],
            device_id=(step, head, blk),
            device_id_type=MESH,
        )

    for s in pairs:
        drift = jnp.dot(
            unpack(attn_buf[s, blk], pair_rows, own_cols),
            wo_buf[blk],
            preferred_element_type=jnp.float32,
        )
        for e in range(1, nb):
            source = (blk + e) % nb
            attn_arrival(s, e).wait_recv()
            drift = drift + jnp.dot(
                unpack(attn_buf[s, source], pair_rows, own_cols),
                wo_buf[source],
                preferred_element_type=jnp.float32,
            )
        drift = drift.reshape(2 * nb, rows, out_cols)
        out_send[2 * s * nb : 2 * (s + 1) * nb] = drift.astype(jnp.bfloat16)
        out_rest[nb + 2 * s * nb : nb + 2 * (s + 1) * nb] = drift
        for i in (s, nh - 1 - s):
            for j in range(nb):
                @pl.when((head != i) | (blk != j))
                def _():
                    out_copy(i, j).start()
    upper = head // (nh // 2)
    own_place = (1 - upper) * 2 * head + upper * (2 * (nh - 1 - head) + 1)
    out_got[me] = jnp.zeros((rows, out_cols), jnp.bfloat16)
    out_rest[0:nb] = jnp.zeros((nb, rows, out_cols), jnp.float32)
    out_rest[blk] = out_rest[nb + own_place * nb + blk]

    for fetch in fetches[4:]:
        fetch.wait()
    coef = coef_table_ref[coef_index_ref[0]]
    for d in range(1, n):
        out_arrival((me + d) % n).wait_recv()

    moved = []
    for c in range(nb):
        total = out_rest[c]
        for h in range(nh):
            total = total + out_got[h * nb + c].astype(jnp.float32)
        gate = mod_buf[
            pl.ds(slot, 1), 2 * width + c * out_cols : 2 * width + (c + 1) * out_cols
        ]
        moved.append(coef * (gate * total))

    carry = pltpu.make_async_remote_copy(
        src_ref=carry_send,
        dst_ref=carry_got,
        send_sem=carry_ss.at[0],
        recv_sem=carry_rs.at[0],
        device_id=(1 - step, head, blk),
        device_id_type=MESH,
    )

    @pl.when(step == 0)
    def _():
        for c in range(nb):
            carry_send[:, c * out_cols : (c + 1) * out_cols] = moved[c].astype(jnp.bfloat16)
        carry.start()
        for c in range(nb):
            cols = slice(c * out_cols, (c + 1) * out_cols)
            out_ref[0, :, cols] = start_ref[:, cols] + moved[c]

    @pl.when(step == 1)
    def _():
        carry.wait_recv()
        for c in range(nb):
            cols = slice(c * out_cols, (c + 1) * out_cols)
            out_ref[0, :, cols] = start_ref[:, cols] + (
                carry_got[:, cols].astype(jnp.float32) + moved[c]
            )

    for i in range(nh):
        @pl.when((i <= head) & (head < nh - 1))
        def _():
            relay(i, 0).wait_send()

        @pl.when((i >= head) & (head > 0))
        def _():
            relay(i, 1).wait_send()

    for e in range(1, nb):
        norm_copy(e).wait_send()
        for p in range(2):
            wo_send(p, e).wait_send()
            wo_part((blk + e) % nb, step, p, fwd_ss, fwd_rs, e).wait_send()
        for s in pairs:
            attn_copy(s, e).wait_send()
    for i in range(nh):
        for way in range(2):
            stage_one(i, way).wait_send()
            stage_two(i, way).wait_send()
    for i in range(nh):
        for j in range(nb):
            @pl.when((head != i) | (blk != j))
            def _():
                out_copy(i, j).wait_send()

    @pl.when(step == 0)
    def _():
        carry.wait_send()


def one_kernel(
    sizes,
    states, start, w_qkv, w_out, q_gain, k_gain, mod_table, step_index, coef_table, coef_index
):
    nh, nb = sizes
    n = nh * nb
    rows, width = start.shape
    depth, _, cols = w_qkv.shape
    own_cols = cols // nb
    out_cols = width // nb
    local_heads = own_cols // HD
    length = rows * n
    packed = nb * rows // 2 * 3 * own_cols // 128
    half16 = jnp.bfloat16
    vmem = pl.BlockSpec(memory_space=pltpu.VMEM)
    hbm = pl.BlockSpec(memory_space=pltpu.HBM)
    dma = pltpu.SemaphoreType.DMA
    return pl.pallas_call(
        functools.partial(whole_kernel, sizes),
        out_shape=jax.ShapeDtypeStruct(states.shape, jnp.float32),
        in_specs=[hbm] * 10,
        out_specs=vmem,
        scratch_shapes=[
            pltpu.VMEM(states.shape, jnp.float32),
            pltpu.VMEM(start.shape, jnp.float32),
            pltpu.VMEM((1, HD), jnp.float32),
            pltpu.VMEM((1, HD), jnp.float32),
            pltpu.SMEM(step_index.shape, jnp.int32),
            pltpu.SMEM(coef_table.shape, jnp.float32),
            pltpu.SMEM(coef_index.shape, jnp.int32),
            pltpu.VMEM((3, depth, cols), half16),
            pltpu.VMEM(mod_table.shape, jnp.float32),
            pltpu.VMEM((nb, rows, depth), half16),
            pltpu.VMEM((n, rows, depth), half16),
            pltpu.VMEM((nh, 2, 2, packed, 128), half16),
            pltpu.VMEM((nh, 2, 2, packed, 128), half16),
            pltpu.VMEM((nh, 2, packed, 128), half16),
            pltpu.VMEM((nh, 2, packed, 128), half16),
            pltpu.VMEM((nh, nb, nb * rows, 3 * own_cols), jnp.float32),
            pltpu.VMEM((nh // 2, nb, 2 * nb * rows * own_cols // 128, 128), half16),
            pltpu.VMEM((nb, own_cols, out_cols), half16),
            pltpu.VMEM((n, rows, out_cols), half16),
            pltpu.VMEM((n, rows, out_cols), half16),
            pltpu.VMEM((nb + n, rows, out_cols), jnp.float32),
            pltpu.VMEM((rows, width), half16),
            pltpu.VMEM((rows, width), half16),
            pltpu.VMEM((local_heads, length, HD), half16),
            pltpu.VMEM((local_heads, length, HD), half16),
            pltpu.VMEM((local_heads, length, HD), half16),
            dma((10,)),
            dma((nb,)), dma((nb,)),
            dma((2 * nh,)), dma((nh,)),
            dma((2 * nh,)), dma((2 * nh,)),
            dma((2 * nh,)), dma((2 * nh,)),
            dma((nb * nh // 2,)), dma((nb * nh // 2,)),
            dma((2 * nb,)), dma((2 * nb,)),
            dma((2 * nb,)), dma((2 * nb,)),
            dma((n,)), dma((n,)),
            dma((1,)), dma((1,)),
        ],
        compiler_params=pltpu.CompilerParams(
            collective_id=0, has_side_effects=True, vmem_limit_bytes=56 * 1024 * 1024
        ),
        name="picard_step",
    )(
        states, start, jnp.transpose(w_qkv, (1, 0, 2)), w_out,
        q_gain[None], k_gain[None], mod_table, step_index, coef_table, coef_index,
    )


def on_device(sizes, *arrays):
    step_count, nh, nb = sizes
    states, start, w_qkv, w_out = arrays[:4]
    rows, width = start.shape
    depth, _, cols = w_qkv.shape
    fits = (
        step_count == 2
        and states.shape[0] == 1
        and nh % 2 == 0
        and nb == 4
        and nh & (nh - 1) == 0
        and rows % 16 == 0
        and cols % (nb * HD) == 0
        and w_out.shape[0] == cols // nb
        and (cols // nb) % 64 == 0
        and depth * nb == width
        and depth % 128 == 0
    )
    if fits:
        return one_kernel((nh, nb), *arrays)
    return general_plan(*arrays)


def solution(mesh):
    in_specs = (
        P("step", ("head", "blk"), None),
        P(("head", "blk"), None),
        P("blk", None, "head"),
        P(("head", "blk"), None),
        P(),
        P(),
        P(),
        P("step"),
        P(),
        P("step"),
    )
    out_specs = P("step", ("head", "blk"), None)
    sizes = (mesh.shape["step"], mesh.shape["head"], mesh.shape["blk"])
    return jax.shard_map(
        functools.partial(on_device, sizes), mesh=mesh, in_specs=in_specs, out_specs=out_specs, check_vma=False
    )
```

```python
import functools

import jax
import jax.numpy as jnp
from jax import lax
from jax.experimental import pallas as pl
from jax.experimental.pallas import tpu as pltpu
from jax.sharding import PartitionSpec as P

HD = 64
MESH = pl.DeviceIdType.MESH


def carried_in(array, axis, join, neutral):
    place = lax.axis_index(axis)
    gathered = lax.all_gather(array.astype(jnp.bfloat16), axis)
    state = jnp.zeros_like(array) + jnp.asarray(neutral, array.dtype)

    def one(step, state):
        return join(state, lax.dynamic_index_in_dim(gathered, step, 0, False).astype(array.dtype))

    return lax.fori_loop(0, place, one, state)


def head_norm(values_in, gains):
    middle = jnp.mean(values_in, axis=-1, keepdims=True)
    spread = jnp.mean((values_in - middle) ** 2, axis=-1, keepdims=True)
    return (values_in - middle) * lax.rsqrt(spread + 1e-06) * gains


def general_plan(
    states, start, w_qkv, w_out, q_gain, k_gain, mod_table, step_index, coef_table, coef_index
):
    width = states.shape[2]
    table_size = mod_table.shape[0]
    slot_ids = jnp.arange(table_size, dtype=jnp.int32)[None, :]
    mod_picks = (step_index[:, None] == slot_ids).astype(jnp.float32)
    coef_picks = (coef_index[:, None] == slot_ids).astype(jnp.float32)
    modulation = jnp.dot(mod_picks, mod_table, precision=lax.Precision.HIGHEST).reshape(
        -1, 3, width
    )
    coefs = jnp.sum(coef_picks * coef_table[None, :], axis=1)
    middle = jnp.mean(states, axis=-1, keepdims=True)
    spread = jnp.mean((states - middle) ** 2, axis=-1, keepdims=True)
    normed = (
        (states - middle) * lax.rsqrt(spread + 1e-05) * (1.0 + modulation[:, 1][:, None, :])
        + modulation[:, 0][:, None, :]
    ).astype(jnp.bfloat16)
    weight_rows = lax.all_gather(w_qkv, "blk", axis=0, tiled=True)
    projected = jnp.einsum(
        "std,dce->stce",
        lax.all_gather(normed, "head", axis=1, tiled=True),
        weight_rows,
        preferred_element_type=jnp.float32,
    )
    step_count = projected.shape[0]
    row_count = projected.shape[1]
    local_heads = projected.shape[3] // HD
    queries = head_norm(
        projected[:, :, 0].reshape(step_count, row_count, local_heads, HD), q_gain
    ).astype(jnp.bfloat16)
    keys_here = head_norm(
        projected[:, :, 1].reshape(step_count, row_count, local_heads, HD), k_gain
    ).astype(jnp.bfloat16)
    values_here = (
        projected[:, :, 2].reshape(step_count, row_count, local_heads, HD).astype(jnp.bfloat16)
    )
    scale_factor = HD ** (-0.5)
    start_best = jnp.full((step_count, local_heads, row_count), -1e30, jnp.float32)
    start_totals = jnp.zeros((step_count, local_heads, row_count), jnp.float32)
    start_accum = jnp.zeros((step_count, local_heads, row_count, HD), jnp.float32)
    best = start_best
    totals = start_totals
    accum = start_accum
    key_piece = lax.all_gather(keys_here, "blk", axis=1, tiled=True)
    value_piece = lax.all_gather(values_here, "blk", axis=1, tiled=True)
    length = key_piece.shape[1]
    for offset in range(0, length, 512):
        stop = min(offset + 512, length)
        key_block = key_piece[:, offset:stop]
        value_block = value_piece[:, offset:stop]
        scores = (
            jnp.einsum("sqhd,skhd->shqk", queries, key_block, preferred_element_type=jnp.float32)
            * scale_factor
        )
        new_best = jnp.maximum(best, jnp.max(scores, axis=-1))
        factor = jnp.exp(best - new_best)
        weights = jnp.exp(scores - new_best[..., None])
        totals = totals * factor + jnp.sum(weights, axis=-1)
        accum = accum * factor[..., None] + jnp.einsum(
            "shqk,skhd->shqd",
            weights.astype(jnp.bfloat16),
            value_block,
            preferred_element_type=jnp.float32,
        )
        best = new_best
    best, totals, accum = (best, totals, accum)
    attn = jnp.transpose(accum / totals[..., None], (0, 2, 1, 3)).reshape(
        step_count, row_count, local_heads * HD
    )
    attn = attn.astype(jnp.bfloat16)
    group_terms = jnp.einsum(
        "srf,fe->sre",
        attn,
        lax.all_gather(w_out, "blk", axis=0, tiled=True),
        preferred_element_type=jnp.float32,
    )
    mixed = lax.psum_scatter(
        group_terms.astype(jnp.bfloat16), "head", scatter_dimension=1, tiled=True
    ).astype(jnp.float32)
    drift = modulation[:, 2][:, None, :] * mixed
    inclusive = jnp.cumsum(coefs[:, None, None] * drift, axis=0)
    own_total = inclusive[-1]
    earlier = carried_in(
        own_total, "step", lambda first, second: first + second, jnp.zeros_like(own_total)
    )
    return start[None] + (earlier[None] + inclusive)


def pack(values):
    rows, cols = values.shape
    tiles = [values[:, at : at + 128] for at in range(0, cols - 127, 128)]
    if cols % 128:
        rest = values[:, cols - 64 :]
        tiles.append(jnp.concatenate([rest[: rows // 2], rest[rows // 2 :]], axis=1))
    return tiles


def unpack(buffer, rows, cols):
    full = cols // 128
    parts = [buffer[t * rows : (t + 1) * rows] for t in range(full)]
    if cols % 128:
        rest = buffer[full * rows :]
        parts.append(jnp.concatenate([rest[:, :64], rest[:, 64:]], axis=0))
    return jnp.concatenate(parts, axis=1)


def whole_kernel(
    sizes,
    states_hbm, start_hbm, w_qkv_ref, w_out_ref, q_gain_hbm, k_gain_hbm, mod_ref,
    step_index_hbm, coef_table_hbm, coef_index_hbm,
    out_ref,
    states_ref, start_ref, q_gain_ref, k_gain_ref, step_index_ref, coef_table_ref, coef_index_ref,
    w_buf, mod_buf, gate_buf, norm_send, norm_got, part_send, part_got, part_own, attn_buf, wo_buf,
    out_send, out_got, carry_send, carry_got, q_buf, k_buf, v_buf,
    local_sem, norm_ss, norm_rs, relay_ss, relay_rs, part_ss, part_rs, attn_ss, attn_rs,
    wo_ss, wo_rs, fwd_ss, fwd_rs, out_ss, out_rs, carry_ss, carry_rs,
):
    nh, nb = sizes
    n = nh * nb
    rows, width = start_ref.shape
    depth = w_buf.shape[1]
    own_cols = w_buf.shape[2] // nb
    out_cols = width // nb
    quarter = own_cols // 4
    local_heads = own_cols // HD
    group_rows = nb * rows
    step = lax.axis_index("step")
    head = lax.axis_index("head")
    blk = lax.axis_index("blk")
    me = head * nb + blk

    fetches = [
        pltpu.make_async_copy(source, target, local_sem.at[3 + place])
        for place, (source, target) in enumerate(
            (
                (states_hbm, states_ref),
                (step_index_hbm, step_index_ref),
                (q_gain_hbm, q_gain_ref),
                (k_gain_hbm, k_gain_ref),
                (coef_index_hbm, coef_index_ref),
                (coef_table_hbm, coef_table_ref),
                (start_hbm, start_ref),
            )
        )
    ]
    for fetch in fetches[:2]:
        fetch.start()
    mod_copy = pltpu.make_async_copy(
        mod_ref.at[:, 0 : 2 * width], mod_buf, local_sem.at[0]
    )
    gate_copy = pltpu.make_async_copy(
        mod_ref.at[:, 2 * width :], gate_buf, local_sem.at[10]
    )
    mod_copy.start()
    for fetch in fetches[2:]:
        fetch.start()
    w_copy = pltpu.make_async_copy(w_qkv_ref, w_buf, local_sem.at[1])
    wo_copy = pltpu.make_async_copy(
        w_out_ref.at[:, pl.ds(pl.multiple_of(blk * out_cols, 128), out_cols)],
        wo_buf.at[blk],
        local_sem.at[2],
    )
    wo_copy.start()

    barrier = pltpu.get_barrier_semaphore()
    for e in range(1, nb):
        pl.semaphore_signal(
            barrier, inc=1, device_id=(step, head, (blk + e) % nb), device_id_type=MESH
        )
    pl.semaphore_signal(barrier, inc=1, device_id=(1 - step, head, blk), device_id_type=MESH)

    @pl.when(head > 0)
    def _():
        pl.semaphore_signal(barrier, inc=1, device_id=(step, head - 1, blk), device_id_type=MESH)

    @pl.when(head < nh - 1)
    def _():
        pl.semaphore_signal(barrier, inc=1, device_id=(step, head + 1, blk), device_id_type=MESH)

    fetches[0].wait()
    current = states_ref[0]
    middle = jnp.mean(current, axis=-1, keepdims=True)
    spread = jnp.mean((current - middle) ** 2, axis=-1, keepdims=True)
    fetches[1].wait()
    mod_copy.wait()
    w_copy.start()
    gate_copy.start()
    slot = step_index_ref[0]
    shift = mod_buf[pl.ds(slot, 1), 0:width]
    scale = mod_buf[pl.ds(slot, 1), width : 2 * width]
    normed = (
        (current - middle) * lax.rsqrt(spread + 1e-05) * (1.0 + scale) + shift
    ).astype(jnp.bfloat16)
    for c in range(nb):
        norm_send[c] = normed[:, c * depth : (c + 1) * depth]
    norm_got[me] = norm_send[blk]
    pl.semaphore_wait(barrier, nb + jnp.minimum(head, 1) + jnp.minimum(nh - 1 - head, 1))

    def norm_copy(e):
        there = (blk + e) % nb
        return pltpu.make_async_remote_copy(
            src_ref=norm_send.at[there],
            dst_ref=norm_got.at[me],
            send_sem=norm_ss.at[e],
            recv_sem=norm_rs.at[blk],
            device_id=(step, head, there),
            device_id_type=MESH,
        )

    def norm_arrival(e):
        source = (blk + e) % nb
        return pltpu.make_async_remote_copy(
            src_ref=norm_send.at[0],
            dst_ref=norm_got.at[head * nb + source],
            send_sem=norm_ss.at[0],
            recv_sem=norm_rs.at[source],
            device_id=(step, head, blk),
            device_id_type=MESH,
        )

    def relay(origin, way):
        place = norm_got.at[origin]
        return pltpu.make_async_remote_copy(
            src_ref=place,
            dst_ref=place,
            send_sem=relay_ss.at[way * n + origin],
            recv_sem=relay_rs.at[origin],
            device_id=(step, head + 1 - 2 * way, blk),
            device_id_type=MESH,
        )

    def upward(origin):
        @pl.when(head < nh - 1)
        def _():
            relay(origin, 0).start()

    def downward(origin):
        @pl.when(head > 0)
        def _():
            relay(origin, 1).start()

    for e in range(1, nb):
        norm_copy(e).start()
    upward(me)
    downward(me)

    def wo_rows(which, p):
        return pl.ds(pl.multiple_of((2 * which + p) * quarter, 16), quarter)

    def wo_send(p, e):
        there = (blk + e) % nb
        return pltpu.make_async_remote_copy(
            src_ref=w_out_ref.at[
                wo_rows(step, p), pl.ds(pl.multiple_of(there * out_cols, 128), out_cols)
            ],
            dst_ref=wo_buf.at[blk, wo_rows(step, p)],
            send_sem=wo_ss.at[p * nb + e],
            recv_sem=wo_rs.at[p * nb + blk],
            device_id=(step, head, there),
            device_id_type=MESH,
        )

    def wo_part(source, which, p, sems, rsems, e):
        place = wo_buf.at[source, wo_rows(which, p)]
        return pltpu.make_async_remote_copy(
            src_ref=place,
            dst_ref=place,
            send_sem=sems.at[p * nb + e],
            recv_sem=rsems.at[p * nb + source],
            device_id=(1 - step, head, blk),
            device_id_type=MESH,
        )

    def wo_pass(p):
        for e in range(1, nb):
            source = (blk + e) % nb
            wo_part(source, step, p, wo_ss, wo_rs, 0).wait_recv()
            wo_part(source, step, p, fwd_ss, fwd_rs, e).start()

    for e in range(1, nb):
        wo_send(0, e).start()

    def part_copy(i, e):
        there = (blk + e) % nb
        return pltpu.make_async_remote_copy(
            src_ref=part_send.at[i, there],
            dst_ref=part_got.at[i, blk],
            send_sem=part_ss.at[i * nb + e],
            recv_sem=part_rs.at[i * nb + blk],
            device_id=(step, head, there),
            device_id_type=MESH,
        )

    def part_arrival(i, e):
        source = (blk + e) % nb
        return pltpu.make_async_remote_copy(
            src_ref=part_send.at[i, 0],
            dst_ref=part_got.at[i, source],
            send_sem=part_ss.at[0],
            recv_sem=part_rs.at[i * nb + source],
            device_id=(step, head, blk),
            device_id_type=MESH,
        )

    for e in range(1, nb):
        norm_arrival(e).wait_recv()
        upward(head * nb + (blk + e) % nb)
        downward(head * nb + (blk + e) % nb)
    w_copy.wait()

    def project(i):
        tokens = norm_got[pl.ds(i * nb, nb)].reshape(group_rows, depth)
        terms = [
            jnp.dot(tokens, w_buf[c], preferred_element_type=jnp.float32) for c in range(3)
        ]
        for c in range(nb):
            share = jnp.concatenate(
                [term[:, c * own_cols : (c + 1) * own_cols] for term in terms], axis=1
            )

            @pl.when(blk == c)
            def _():
                part_own[i] = share

            @pl.when(blk != c)
            def _():
                packed = pack(share.astype(jnp.bfloat16))
                for t, tile in enumerate(packed):
                    part_send[i, c, t * group_rows : t * group_rows + tile.shape[0]] = tile

        for e in range(1, nb):
            part_copy(i, e).start()

    project(head)
    for e in range(1, nb):
        wo_send(1, e).start()

    def further(d, carried):
        low, high = head - d, head + d

        for e in range(nb):
            place = (blk + e) % nb

            @pl.when(low >= 0)
            def _():
                relay(low * nb + place, 0).wait_recv()
                upward(low * nb + place)

            @pl.when(high < nh)
            def _():
                relay(high * nb + place, 0).wait_recv()
                downward(high * nb + place)

        @pl.when(low >= 0)
        def _():
            project(low)

        @pl.when(high < nh)
        def _():
            project(high)

        return carried

    lax.fori_loop(1, nh, further, 0)

    wo_pass(0)
    wo_pass(1)

    def head_parts(values, gains):
        center = jnp.mean(values, axis=-1, keepdims=True)
        width_sq = jnp.mean((values - center) ** 2, axis=-1, keepdims=True)
        return (values - center) * lax.rsqrt(width_sq + 1e-06) * gains

    fetches[2].wait()
    fetches[3].wait()
    q_gain = q_gain_ref[...] * HD ** (-0.5)

    def finish(i):
        total = part_own[i]
        for e in range(1, nb):
            part_arrival(i, e).wait_recv()
            total = total + unpack(
                part_got.at[i, (blk + e) % nb], group_rows, 3 * own_cols
            ).astype(jnp.float32)
        upper = i // (nh // 2)
        place = (1 - upper) * 2 * i + upper * (2 * (nh - 1 - i) + 1)
        here = pl.ds(pl.multiple_of(place * group_rows, group_rows), group_rows)
        for g in range(local_heads):
            at = g * HD
            q_buf[g, here] = head_parts(total[:, at : at + HD], q_gain).astype(
                jnp.bfloat16
            )
            at += own_cols
            k_buf[g, here] = head_parts(total[:, at : at + HD], k_gain_ref[...]).astype(
                jnp.bfloat16
            )
            at += own_cols
            v_buf[g, here] = total[:, at : at + HD].astype(jnp.bfloat16)

    orders = [sorted(range(nh), key=lambda o: (abs(o - h), o)) for h in range(nh)]
    for i in range(nh):
        place = orders[0][i]
        for h in range(1, nh):
            place = jnp.where(head == h, orders[h][i], place)
        finish(place)

    def attn_copy(s, e):
        there = (blk + e) % nb
        return pltpu.make_async_remote_copy(
            src_ref=attn_buf.at[s, blk],
            dst_ref=attn_buf.at[s, blk],
            send_sem=attn_ss.at[s * nb + e],
            recv_sem=attn_rs.at[s * nb + blk],
            device_id=(step, head, there),
            device_id_type=MESH,
        )

    def attn_arrival(s, e):
        source = (blk + e) % nb
        return pltpu.make_async_remote_copy(
            src_ref=attn_buf.at[s, blk],
            dst_ref=attn_buf.at[s, source],
            send_sem=attn_ss.at[0],
            recv_sem=attn_rs.at[s * nb + source],
            device_id=(step, head, blk),
            device_id_type=MESH,
        )

    pair_rows = 2 * group_rows
    pairs = range(nh // 2)
    for s in pairs:
        here = slice(s * pair_rows, (s + 1) * pair_rows)
        mixed = []
        for g in range(local_heads):
            scores = lax.dot_general(
                q_buf[g, here],
                k_buf[g],
                (((1,), (1,)), ((), ())),
                preferred_element_type=jnp.float32,
            )
            weights = jnp.exp(scores - jnp.max(scores, axis=-1, keepdims=True))
            totals = jnp.sum(weights, axis=-1, keepdims=True)
            value = jnp.dot(
                weights.astype(jnp.bfloat16), v_buf[g], preferred_element_type=jnp.float32
            )
            mixed.append((value / totals).astype(jnp.bfloat16))
        for t, tile in enumerate(pack(jnp.concatenate(mixed, axis=1))):
            attn_buf[s, blk, t * pair_rows : t * pair_rows + tile.shape[0]] = tile
        for e in range(1, nb):
            attn_copy(s, e).start()

    wo_copy.wait()
    for e in range(1, nb):
        source = (blk + e) % nb
        for p in range(2):
            wo_part(source, 1 - step, p, fwd_ss, fwd_rs, 0).wait_recv()

    def out_place(i):
        return 2 * i if i < nh // 2 else 2 * (nh - 1 - i) + 1

    def out_copy(i, j):
        return pltpu.make_async_remote_copy(
            src_ref=out_send.at[out_place(i) * nb + j],
            dst_ref=out_got.at[me],
            send_sem=out_ss.at[i * nb + j],
            recv_sem=out_rs.at[me],
            device_id=(step, i, j),
            device_id_type=MESH,
        )

    def out_arrival(source):
        return pltpu.make_async_remote_copy(
            src_ref=out_send.at[0],
            dst_ref=out_got.at[source],
            send_sem=out_ss.at[0],
            recv_sem=out_rs.at[source],
            device_id=(step, head, blk),
            device_id_type=MESH,
        )

    for s in pairs:
        drift = jnp.dot(
            unpack(attn_buf[s, blk], pair_rows, own_cols),
            wo_buf[blk],
            preferred_element_type=jnp.float32,
        )
        for e in range(1, nb):
            source = (blk + e) % nb
            attn_arrival(s, e).wait_recv()
            drift = drift + jnp.dot(
                unpack(attn_buf[s, source], pair_rows, own_cols),
                wo_buf[source],
                preferred_element_type=jnp.float32,
            )
        out_send[2 * s * nb : 2 * (s + 1) * nb] = drift.astype(jnp.bfloat16).reshape(
            2 * nb, rows, out_cols
        )
        for i in (s, nh - 1 - s):
            for j in range(nb):
                @pl.when((head != i) | (blk != j))
                def _():
                    out_copy(i, j).start()
    upper = head // (nh // 2)
    own_place = (1 - upper) * 2 * head + upper * (2 * (nh - 1 - head) + 1)
    out_got[me] = out_send[own_place * nb + blk]

    for fetch in fetches[4:]:
        fetch.wait()
    gate_copy.wait()
    coef = coef_table_ref[coef_index_ref[0]]
    for d in range(1, n):
        out_arrival((me + d) % n).wait_recv()

    moved = []
    for c in range(nb):
        total = out_got[c].astype(jnp.float32)
        for h in range(1, nh):
            total = total + out_got[h * nb + c].astype(jnp.float32)
        gate = gate_buf[pl.ds(slot, 1), c * out_cols : (c + 1) * out_cols]
        moved.append(coef * (gate * total))

    carry = pltpu.make_async_remote_copy(
        src_ref=carry_send,
        dst_ref=carry_got,
        send_sem=carry_ss.at[0],
        recv_sem=carry_rs.at[0],
        device_id=(1 - step, head, blk),
        device_id_type=MESH,
    )

    @pl.when(step == 0)
    def _():
        for c in range(nb):
            carry_send[:, c * out_cols : (c + 1) * out_cols] = moved[c].astype(jnp.bfloat16)
        carry.start()
        for c in range(nb):
            cols = slice(c * out_cols, (c + 1) * out_cols)
            out_ref[0, :, cols] = start_ref[:, cols] + moved[c]

    @pl.when(step == 1)
    def _():
        carry.wait_recv()
        for c in range(nb):
            cols = slice(c * out_cols, (c + 1) * out_cols)
            out_ref[0, :, cols] = start_ref[:, cols] + (
                carry_got[:, cols].astype(jnp.float32) + moved[c]
            )

    for i in range(nh):
        @pl.when((i <= head) & (head < nh - 1))
        def _():
            for j in range(nb):
                relay(i * nb + j, 0).wait_send()

        @pl.when((i >= head) & (head > 0))
        def _():
            for j in range(nb):
                relay(i * nb + j, 1).wait_send()

    for e in range(1, nb):
        norm_copy(e).wait_send()
        for p in range(2):
            wo_send(p, e).wait_send()
            wo_part((blk + e) % nb, step, p, fwd_ss, fwd_rs, e).wait_send()
        for s in pairs:
            attn_copy(s, e).wait_send()
        for i in range(nh):
            part_copy(i, e).wait_send()
    for i in range(nh):
        for j in range(nb):
            @pl.when((head != i) | (blk != j))
            def _():
                out_copy(i, j).wait_send()

    @pl.when(step == 0)
    def _():
        carry.wait_send()


def one_kernel(
    sizes,
    states, start, w_qkv, w_out, q_gain, k_gain, mod_table, step_index, coef_table, coef_index
):
    nh, nb = sizes
    n = nh * nb
    rows, width = start.shape
    depth, _, cols = w_qkv.shape
    own_cols = cols // nb
    out_cols = width // nb
    local_heads = own_cols // HD
    length = rows * n
    half16 = jnp.bfloat16
    vmem = pl.BlockSpec(memory_space=pltpu.VMEM)
    hbm = pl.BlockSpec(memory_space=pltpu.HBM)
    dma = pltpu.SemaphoreType.DMA
    return pl.pallas_call(
        functools.partial(whole_kernel, sizes),
        out_shape=jax.ShapeDtypeStruct(states.shape, jnp.float32),
        in_specs=[hbm] * 10,
        out_specs=vmem,
        scratch_shapes=[
            pltpu.VMEM(states.shape, jnp.float32),
            pltpu.VMEM(start.shape, jnp.float32),
            pltpu.VMEM((1, HD), jnp.float32),
            pltpu.VMEM((1, HD), jnp.float32),
            pltpu.SMEM(step_index.shape, jnp.int32),
            pltpu.SMEM(coef_table.shape, jnp.float32),
            pltpu.SMEM(coef_index.shape, jnp.int32),
            pltpu.VMEM((3, depth, cols), half16),
            pltpu.VMEM((mod_table.shape[0], 2 * width), jnp.float32),
            pltpu.VMEM((mod_table.shape[0], width), jnp.float32),
            pltpu.VMEM((nb, rows, depth), half16),
            pltpu.VMEM((n, rows, depth), half16),
            pltpu.VMEM((nh, nb, nb * rows * 3 * own_cols // 128, 128), half16),
            pltpu.VMEM((nh, nb, nb * rows * 3 * own_cols // 128, 128), half16),
            pltpu.VMEM((nh, nb * rows, 3 * own_cols), jnp.float32),
            pltpu.VMEM((nh // 2, nb, 2 * nb * rows * own_cols // 128, 128), half16),
            pltpu.VMEM((nb, own_cols, out_cols), half16),
            pltpu.VMEM((n, rows, out_cols), half16),
            pltpu.VMEM((n, rows, out_cols), half16),
            pltpu.VMEM((rows, width), half16),
            pltpu.VMEM((rows, width), half16),
            pltpu.VMEM((local_heads, length, HD), half16),
            pltpu.VMEM((local_heads, length, HD), half16),
            pltpu.VMEM((local_heads, length, HD), half16),
            dma((11,)),
            dma((nb,)), dma((nb,)),
            dma((2 * n,)), dma((n,)),
            dma((n,)), dma((n,)),
            dma((nb * nh // 2,)), dma((nb * nh // 2,)),
            dma((2 * nb,)), dma((2 * nb,)),
            dma((2 * nb,)), dma((2 * nb,)),
            dma((n,)), dma((n,)),
            dma((1,)), dma((1,)),
        ],
        compiler_params=pltpu.CompilerParams(
            collective_id=0, has_side_effects=True, vmem_limit_bytes=56 * 1024 * 1024
        ),
        name="picard_step",
    )(
        states, start, jnp.transpose(w_qkv, (1, 0, 2)), w_out,
        q_gain[None], k_gain[None], mod_table, step_index, coef_table, coef_index,
    )


def on_device(sizes, *arrays):
    step_count, nh, nb = sizes
    states, start, w_qkv, w_out = arrays[:4]
    rows, width = start.shape
    depth, _, cols = w_qkv.shape
    fits = (
        step_count == 2
        and states.shape[0] == 1
        and nh % 2 == 0
        and nh & (nh - 1) == 0
        and rows % 16 == 0
        and cols % (nb * HD) == 0
        and w_out.shape[0] == cols // nb
        and (cols // nb) % 64 == 0
        and depth * nb == width
        and depth % 128 == 0
    )
    if fits:
        return one_kernel((nh, nb), *arrays)
    return general_plan(*arrays)


def solution(mesh):
    in_specs = (
        P("step", ("head", "blk"), None),
        P(("head", "blk"), None),
        P("blk", None, "head"),
        P(("head", "blk"), None),
        P(),
        P(),
        P(),
        P("step"),
        P(),
        P("step"),
    )
    out_specs = P("step", ("head", "blk"), None)
    sizes = (mesh.shape["step"], mesh.shape["head"], mesh.shape["blk"])
    return jax.shard_map(
        functools.partial(on_device, sizes), mesh=mesh, in_specs=in_specs, out_specs=out_specs, check_vma=False
    )
```

```python
import functools

import jax
import jax.numpy as jnp
from jax import lax
from jax.experimental import pallas as pl
from jax.experimental.pallas import tpu as pltpu
from jax.sharding import PartitionSpec as P

HD = 64
MESH = pl.DeviceIdType.MESH


def carried_in(array, axis, join, neutral):
    place = lax.axis_index(axis)
    gathered = lax.all_gather(array.astype(jnp.bfloat16), axis)
    state = jnp.zeros_like(array) + jnp.asarray(neutral, array.dtype)

    def one(step, state):
        return join(state, lax.dynamic_index_in_dim(gathered, step, 0, False).astype(array.dtype))

    return lax.fori_loop(0, place, one, state)


def head_norm(values_in, gains):
    middle = jnp.mean(values_in, axis=-1, keepdims=True)
    spread = jnp.mean((values_in - middle) ** 2, axis=-1, keepdims=True)
    return (values_in - middle) * lax.rsqrt(spread + 1e-06) * gains


def general_plan(
    states, start, w_qkv, w_out, q_gain, k_gain, mod_table, step_index, coef_table, coef_index
):
    width = states.shape[2]
    table_size = mod_table.shape[0]
    slot_ids = jnp.arange(table_size, dtype=jnp.int32)[None, :]
    mod_picks = (step_index[:, None] == slot_ids).astype(jnp.float32)
    coef_picks = (coef_index[:, None] == slot_ids).astype(jnp.float32)
    modulation = jnp.dot(mod_picks, mod_table, precision=lax.Precision.HIGHEST).reshape(
        -1, 3, width
    )
    coefs = jnp.sum(coef_picks * coef_table[None, :], axis=1)
    middle = jnp.mean(states, axis=-1, keepdims=True)
    spread = jnp.mean((states - middle) ** 2, axis=-1, keepdims=True)
    normed = (
        (states - middle) * lax.rsqrt(spread + 1e-05) * (1.0 + modulation[:, 1][:, None, :])
        + modulation[:, 0][:, None, :]
    ).astype(jnp.bfloat16)
    weight_rows = lax.all_gather(w_qkv, "blk", axis=0, tiled=True)
    projected = jnp.einsum(
        "std,dce->stce",
        lax.all_gather(normed, "head", axis=1, tiled=True),
        weight_rows,
        preferred_element_type=jnp.float32,
    )
    step_count = projected.shape[0]
    row_count = projected.shape[1]
    local_heads = projected.shape[3] // HD
    queries = head_norm(
        projected[:, :, 0].reshape(step_count, row_count, local_heads, HD), q_gain
    ).astype(jnp.bfloat16)
    keys_here = head_norm(
        projected[:, :, 1].reshape(step_count, row_count, local_heads, HD), k_gain
    ).astype(jnp.bfloat16)
    values_here = (
        projected[:, :, 2].reshape(step_count, row_count, local_heads, HD).astype(jnp.bfloat16)
    )
    scale_factor = HD ** (-0.5)
    start_best = jnp.full((step_count, local_heads, row_count), -1e30, jnp.float32)
    start_totals = jnp.zeros((step_count, local_heads, row_count), jnp.float32)
    start_accum = jnp.zeros((step_count, local_heads, row_count, HD), jnp.float32)
    best = start_best
    totals = start_totals
    accum = start_accum
    key_piece = lax.all_gather(keys_here, "blk", axis=1, tiled=True)
    value_piece = lax.all_gather(values_here, "blk", axis=1, tiled=True)
    length = key_piece.shape[1]
    for offset in range(0, length, 512):
        stop = min(offset + 512, length)
        key_block = key_piece[:, offset:stop]
        value_block = value_piece[:, offset:stop]
        scores = (
            jnp.einsum("sqhd,skhd->shqk", queries, key_block, preferred_element_type=jnp.float32)
            * scale_factor
        )
        new_best = jnp.maximum(best, jnp.max(scores, axis=-1))
        factor = jnp.exp(best - new_best)
        weights = jnp.exp(scores - new_best[..., None])
        totals = totals * factor + jnp.sum(weights, axis=-1)
        accum = accum * factor[..., None] + jnp.einsum(
            "shqk,skhd->shqd",
            weights.astype(jnp.bfloat16),
            value_block,
            preferred_element_type=jnp.float32,
        )
        best = new_best
    best, totals, accum = (best, totals, accum)
    attn = jnp.transpose(accum / totals[..., None], (0, 2, 1, 3)).reshape(
        step_count, row_count, local_heads * HD
    )
    attn = attn.astype(jnp.bfloat16)
    group_terms = jnp.einsum(
        "srf,fe->sre",
        attn,
        lax.all_gather(w_out, "blk", axis=0, tiled=True),
        preferred_element_type=jnp.float32,
    )
    mixed = lax.psum_scatter(
        group_terms.astype(jnp.bfloat16), "head", scatter_dimension=1, tiled=True
    ).astype(jnp.float32)
    drift = modulation[:, 2][:, None, :] * mixed
    inclusive = jnp.cumsum(coefs[:, None, None] * drift, axis=0)
    own_total = inclusive[-1]
    earlier = carried_in(
        own_total, "step", lambda first, second: first + second, jnp.zeros_like(own_total)
    )
    return start[None] + (earlier[None] + inclusive)


def pack(values):
    rows, cols = values.shape
    tiles = [values[:, at : at + 128] for at in range(0, cols - 127, 128)]
    if cols % 128:
        rest = values[:, cols - 64 :]
        tiles.append(jnp.concatenate([rest[: rows // 2], rest[rows // 2 :]], axis=1))
    return tiles


def unpack(buffer, rows, cols):
    full = cols // 128
    parts = [buffer[t * rows : (t + 1) * rows] for t in range(full)]
    if cols % 128:
        rest = buffer[full * rows :]
        parts.append(jnp.concatenate([rest[:, :64], rest[:, 64:]], axis=0))
    return jnp.concatenate(parts, axis=1)


def whole_kernel(
    sizes,
    states_hbm, start_hbm, w_qkv_ref, w_out_ref, q_gain_hbm, k_gain_hbm, mod_ref,
    step_index_hbm, coef_table_hbm, coef_index_hbm,
    out_ref,
    states_ref, start_ref, q_gain_ref, k_gain_ref, step_index_ref, coef_table_ref, coef_index_ref,
    w_buf, mod_buf, gate_buf, norm_send, norm_got, part_send, part_got, part_own, attn_buf, wo_buf,
    out_send, out_got, carry_send, carry_got, q_buf, k_buf, v_buf,
    local_sem, norm_ss, norm_rs, relay_ss, relay_rs, part_ss, part_rs, attn_ss, attn_rs,
    wo_ss, wo_rs, fwd_ss, fwd_rs, out_ss, out_rs, carry_ss, carry_rs,
):
    nh, nb = sizes
    n = nh * nb
    rows, width = start_ref.shape
    depth = w_buf.shape[1]
    own_cols = w_buf.shape[2] // nb
    out_cols = width // nb
    quarter = own_cols // 4
    local_heads = own_cols // HD
    group_rows = nb * rows
    step = lax.axis_index("step")
    head = lax.axis_index("head")
    blk = lax.axis_index("blk")
    me = head * nb + blk

    fetches = [
        pltpu.make_async_copy(source, target, local_sem.at[3 + place])
        for place, (source, target) in enumerate(
            (
                (states_hbm, states_ref),
                (step_index_hbm, step_index_ref),
                (q_gain_hbm, q_gain_ref),
                (k_gain_hbm, k_gain_ref),
                (coef_index_hbm, coef_index_ref),
                (coef_table_hbm, coef_table_ref),
                (start_hbm, start_ref),
            )
        )
    ]
    for fetch in fetches[:2]:
        fetch.start()
    mod_copy = pltpu.make_async_copy(
        mod_ref.at[:, 0 : 2 * width], mod_buf, local_sem.at[0]
    )
    gate_copy = pltpu.make_async_copy(
        mod_ref.at[:, 2 * width :], gate_buf, local_sem.at[10]
    )
    mod_copy.start()
    for fetch in fetches[2:]:
        fetch.start()
    w_copy = pltpu.make_async_copy(w_qkv_ref, w_buf, local_sem.at[1])
    wo_copy = pltpu.make_async_copy(
        w_out_ref.at[:, pl.ds(pl.multiple_of(blk * out_cols, 128), out_cols)],
        wo_buf.at[blk],
        local_sem.at[2],
    )
    wo_copy.start()

    barrier = pltpu.get_barrier_semaphore()
    for e in range(1, nb):
        pl.semaphore_signal(
            barrier, inc=1, device_id=(step, head, (blk + e) % nb), device_id_type=MESH
        )
    pl.semaphore_signal(barrier, inc=1, device_id=(1 - step, head, blk), device_id_type=MESH)

    @pl.when(head > 0)
    def _():
        pl.semaphore_signal(barrier, inc=1, device_id=(step, head - 1, blk), device_id_type=MESH)

    @pl.when(head < nh - 1)
    def _():
        pl.semaphore_signal(barrier, inc=1, device_id=(step, head + 1, blk), device_id_type=MESH)

    fetches[0].wait()
    current = states_ref[0]
    middle = jnp.mean(current, axis=-1, keepdims=True)
    spread = jnp.mean((current - middle) ** 2, axis=-1, keepdims=True)
    fetches[1].wait()
    mod_copy.wait()
    w_copy.start()
    gate_copy.start()
    slot = step_index_ref[0]
    shift = mod_buf[pl.ds(slot, 1), 0:width]
    scale = mod_buf[pl.ds(slot, 1), width : 2 * width]
    normed = (
        (current - middle) * lax.rsqrt(spread + 1e-05) * (1.0 + scale) + shift
    ).astype(jnp.bfloat16)
    for c in range(nb):
        norm_send[c] = normed[:, c * depth : (c + 1) * depth]
    norm_got[me] = norm_send[blk]
    pl.semaphore_wait(barrier, nb + jnp.minimum(head, 1) + jnp.minimum(nh - 1 - head, 1))

    def norm_copy(e):
        there = (blk + e) % nb
        return pltpu.make_async_remote_copy(
            src_ref=norm_send.at[there],
            dst_ref=norm_got.at[me],
            send_sem=norm_ss.at[e],
            recv_sem=norm_rs.at[blk],
            device_id=(step, head, there),
            device_id_type=MESH,
        )

    def norm_arrival(e):
        source = (blk + e) % nb
        return pltpu.make_async_remote_copy(
            src_ref=norm_send.at[0],
            dst_ref=norm_got.at[head * nb + source],
            send_sem=norm_ss.at[0],
            recv_sem=norm_rs.at[source],
            device_id=(step, head, blk),
            device_id_type=MESH,
        )

    def relay(origin, way):
        place = norm_got.at[origin]
        return pltpu.make_async_remote_copy(
            src_ref=place,
            dst_ref=place,
            send_sem=relay_ss.at[way * n + origin],
            recv_sem=relay_rs.at[origin],
            device_id=(step, head + 1 - 2 * way, blk),
            device_id_type=MESH,
        )

    def upward(origin):
        @pl.when(head < nh - 1)
        def _():
            relay(origin, 0).start()

    def downward(origin):
        @pl.when(head > 0)
        def _():
            relay(origin, 1).start()

    for e in range(1, nb):
        norm_copy(e).start()
    upward(me)
    downward(me)

    def wo_rows(which, p):
        return pl.ds(pl.multiple_of((2 * which + p) * quarter, 16), quarter)

    def wo_send(p, e):
        there = (blk + e) % nb
        return pltpu.make_async_remote_copy(
            src_ref=w_out_ref.at[
                wo_rows(step, p), pl.ds(pl.multiple_of(there * out_cols, 128), out_cols)
            ],
            dst_ref=wo_buf.at[blk, wo_rows(step, p)],
            send_sem=wo_ss.at[p * nb + e],
            recv_sem=wo_rs.at[p * nb + blk],
            device_id=(step, head, there),
            device_id_type=MESH,
        )

    def wo_part(source, which, p, sems, rsems, e):
        place = wo_buf.at[source, wo_rows(which, p)]
        return pltpu.make_async_remote_copy(
            src_ref=place,
            dst_ref=place,
            send_sem=sems.at[p * nb + e],
            recv_sem=rsems.at[p * nb + source],
            device_id=(1 - step, head, blk),
            device_id_type=MESH,
        )

    def wo_pass(p):
        for e in range(1, nb):
            source = (blk + e) % nb
            wo_part(source, step, p, wo_ss, wo_rs, 0).wait_recv()
            wo_part(source, step, p, fwd_ss, fwd_rs, e).start()

    for e in range(1, nb):
        wo_send(0, e).start()

    def part_copy(i, e):
        there = (blk + e) % nb
        return pltpu.make_async_remote_copy(
            src_ref=part_send.at[i, there],
            dst_ref=part_got.at[i, blk],
            send_sem=part_ss.at[i * nb + e],
            recv_sem=part_rs.at[i * nb + blk],
            device_id=(step, head, there),
            device_id_type=MESH,
        )

    def part_arrival(i, e):
        source = (blk + e) % nb
        return pltpu.make_async_remote_copy(
            src_ref=part_send.at[i, 0],
            dst_ref=part_got.at[i, source],
            send_sem=part_ss.at[0],
            recv_sem=part_rs.at[i * nb + source],
            device_id=(step, head, blk),
            device_id_type=MESH,
        )

    for e in range(1, nb):
        norm_arrival(e).wait_recv()
        upward(head * nb + (blk + e) % nb)
        downward(head * nb + (blk + e) % nb)
    w_copy.wait()

    def project(i):
        tokens = norm_got[pl.ds(i * nb, nb)].reshape(group_rows, depth)
        terms = [
            jnp.dot(tokens, w_buf[c], preferred_element_type=jnp.float32) for c in range(3)
        ]
        for c in range(nb):
            share = jnp.concatenate(
                [term[:, c * own_cols : (c + 1) * own_cols] for term in terms], axis=1
            )

            @pl.when(blk == c)
            def _():
                part_own[i] = share

            @pl.when(blk != c)
            def _():
                packed = pack(share.astype(jnp.bfloat16))
                for t, tile in enumerate(packed):
                    part_send[i, c, t * group_rows : t * group_rows + tile.shape[0]] = tile

        for e in range(1, nb):
            part_copy(i, e).start()

    project(head)
    for e in range(1, nb):
        wo_send(1, e).start()

    def further(d, carried):
        low, high = head - d, head + d

        for e in range(nb):
            place = (blk + e) % nb

            @pl.when(low >= 0)
            def _():
                relay(low * nb + place, 0).wait_recv()
                upward(low * nb + place)

            @pl.when(high < nh)
            def _():
                relay(high * nb + place, 0).wait_recv()
                downward(high * nb + place)

        @pl.when(low >= 0)
        def _():
            project(low)

        @pl.when(high < nh)
        def _():
            project(high)

        return carried

    lax.fori_loop(1, nh, further, 0)

    wo_pass(0)
    wo_pass(1)

    def head_parts(values, gains):
        center = jnp.mean(values, axis=-1, keepdims=True)
        width_sq = jnp.mean((values - center) ** 2, axis=-1, keepdims=True)
        return (values - center) * lax.rsqrt(width_sq + 1e-06) * gains

    fetches[2].wait()
    fetches[3].wait()
    q_gain = q_gain_ref[...] * HD ** (-0.5)

    def finish(i):
        total = part_own[i]
        for e in range(1, nb):
            part_arrival(i, e).wait_recv()
            total = total + unpack(
                part_got.at[i, (blk + e) % nb], group_rows, 3 * own_cols
            ).astype(jnp.float32)
        upper = i // (nh // 2)
        place = (1 - upper) * 2 * i + upper * (2 * (nh - 1 - i) + 1)
        here = pl.ds(pl.multiple_of(place * group_rows, group_rows), group_rows)
        for g in range(local_heads):
            at = g * HD
            q_buf[g, here] = head_parts(total[:, at : at + HD], q_gain).astype(
                jnp.bfloat16
            )
            at += own_cols
            k_buf[g, here] = head_parts(total[:, at : at + HD], k_gain_ref[...]).astype(
                jnp.bfloat16
            )
            at += own_cols
            v_buf[g, here] = total[:, at : at + HD].astype(jnp.bfloat16)

    orders = [sorted(range(nh), key=lambda o: (abs(o - h), o)) for h in range(nh)]
    for i in range(nh):
        place = orders[0][i]
        for h in range(1, nh):
            place = jnp.where(head == h, orders[h][i], place)
        finish(place)

    def attn_copy(s, e):
        there = (blk + e) % nb
        return pltpu.make_async_remote_copy(
            src_ref=attn_buf.at[s, blk],
            dst_ref=attn_buf.at[s, blk],
            send_sem=attn_ss.at[s * nb + e],
            recv_sem=attn_rs.at[s * nb + blk],
            device_id=(step, head, there),
            device_id_type=MESH,
        )

    def attn_arrival(s, e):
        source = (blk + e) % nb
        return pltpu.make_async_remote_copy(
            src_ref=attn_buf.at[s, blk],
            dst_ref=attn_buf.at[s, source],
            send_sem=attn_ss.at[0],
            recv_sem=attn_rs.at[s * nb + source],
            device_id=(step, head, blk),
            device_id_type=MESH,
        )

    pair_rows = 2 * group_rows
    pairs = range(nh // 2)
    for s in pairs:
        here = slice(s * pair_rows, (s + 1) * pair_rows)
        mixed = []
        for g in range(local_heads):
            scores = lax.dot_general(
                q_buf[g, here],
                k_buf[g],
                (((1,), (1,)), ((), ())),
                preferred_element_type=jnp.float32,
            )
            weights = jnp.exp(scores - jnp.max(scores, axis=-1, keepdims=True))
            totals = jnp.sum(weights, axis=-1, keepdims=True)
            value = jnp.dot(
                weights.astype(jnp.bfloat16), v_buf[g], preferred_element_type=jnp.float32
            )
            mixed.append((value / totals).astype(jnp.bfloat16))
        for t, tile in enumerate(pack(jnp.concatenate(mixed, axis=1))):
            attn_buf[s, blk, t * pair_rows : t * pair_rows + tile.shape[0]] = tile
        for e in range(1, nb):
            attn_copy(s, e).start()

    wo_copy.wait()
    for e in range(1, nb):
        source = (blk + e) % nb
        for p in range(2):
            wo_part(source, 1 - step, p, fwd_ss, fwd_rs, 0).wait_recv()

    def out_place(i):
        return 2 * i if i < nh // 2 else 2 * (nh - 1 - i) + 1

    def out_copy(i, j):
        return pltpu.make_async_remote_copy(
            src_ref=out_send.at[out_place(i) * nb + j],
            dst_ref=out_got.at[me],
            send_sem=out_ss.at[i * nb + j],
            recv_sem=out_rs.at[me],
            device_id=(step, i, j),
            device_id_type=MESH,
        )

    def out_arrival(source):
        return pltpu.make_async_remote_copy(
            src_ref=out_send.at[0],
            dst_ref=out_got.at[source],
            send_sem=out_ss.at[0],
            recv_sem=out_rs.at[source],
            device_id=(step, head, blk),
            device_id_type=MESH,
        )

    for s in pairs:
        drift = jnp.dot(
            unpack(attn_buf[s, blk], pair_rows, own_cols),
            wo_buf[blk],
            preferred_element_type=jnp.float32,
        )
        for e in range(1, nb):
            source = (blk + e) % nb
            attn_arrival(s, e).wait_recv()
            drift = drift + jnp.dot(
                unpack(attn_buf[s, source], pair_rows, own_cols),
                wo_buf[source],
                preferred_element_type=jnp.float32,
            )
        out_send[2 * s * nb : 2 * (s + 1) * nb] = drift.astype(jnp.bfloat16).reshape(
            2 * nb, rows, out_cols
        )
        for i in (s, nh - 1 - s):
            for j in range(nb):
                @pl.when((head != i) | (blk != j))
                def _():
                    out_copy(i, j).start()
    upper = head // (nh // 2)
    own_place = (1 - upper) * 2 * head + upper * (2 * (nh - 1 - head) + 1)
    out_got[me] = out_send[own_place * nb + blk]

    for fetch in fetches[4:]:
        fetch.wait()
    gate_copy.wait()
    coef = coef_table_ref[coef_index_ref[0]]

    def carry(c):
        place = (slice(None), slice(c * out_cols, (c + 1) * out_cols))
        return pltpu.make_async_remote_copy(
            src_ref=carry_send.at[place],
            dst_ref=carry_got.at[place],
            send_sem=carry_ss.at[c],
            recv_sem=carry_rs.at[c],
            device_id=(1 - step, head, blk),
            device_id_type=MESH,
        )

    moved = []
    for c in range(nb):
        for h in range(nh):
            @pl.when(me != h * nb + c)
            def _():
                out_arrival(h * nb + c).wait_recv()
        total = out_got[c].astype(jnp.float32)
        for h in range(1, nh):
            total = total + out_got[h * nb + c].astype(jnp.float32)
        gate = gate_buf[pl.ds(slot, 1), c * out_cols : (c + 1) * out_cols]
        moved.append(coef * (gate * total))

        @pl.when(step == 0)
        def _():
            carry_send[:, c * out_cols : (c + 1) * out_cols] = moved[c].astype(jnp.bfloat16)
            carry(c).start()

    for c in range(nb):
        cols = slice(c * out_cols, (c + 1) * out_cols)

        @pl.when(step == 0)
        def _():
            out_ref[0, :, cols] = start_ref[:, cols] + moved[c]

        @pl.when(step == 1)
        def _():
            carry(c).wait_recv()
            out_ref[0, :, cols] = start_ref[:, cols] + (
                carry_got[:, cols].astype(jnp.float32) + moved[c]
            )

    for i in range(nh):
        @pl.when((i <= head) & (head < nh - 1))
        def _():
            for j in range(nb):
                relay(i * nb + j, 0).wait_send()

        @pl.when((i >= head) & (head > 0))
        def _():
            for j in range(nb):
                relay(i * nb + j, 1).wait_send()

    for e in range(1, nb):
        norm_copy(e).wait_send()
        for p in range(2):
            wo_send(p, e).wait_send()
            wo_part((blk + e) % nb, step, p, fwd_ss, fwd_rs, e).wait_send()
        for s in pairs:
            attn_copy(s, e).wait_send()
        for i in range(nh):
            part_copy(i, e).wait_send()
    for i in range(nh):
        for j in range(nb):
            @pl.when((head != i) | (blk != j))
            def _():
                out_copy(i, j).wait_send()

    @pl.when(step == 0)
    def _():
        for c in range(nb):
            carry(c).wait_send()


def one_kernel(
    sizes,
    states, start, w_qkv, w_out, q_gain, k_gain, mod_table, step_index, coef_table, coef_index
):
    nh, nb = sizes
    n = nh * nb
    rows, width = start.shape
    depth, _, cols = w_qkv.shape
    own_cols = cols // nb
    out_cols = width // nb
    local_heads = own_cols // HD
    length = rows * n
    half16 = jnp.bfloat16
    vmem = pl.BlockSpec(memory_space=pltpu.VMEM)
    hbm = pl.BlockSpec(memory_space=pltpu.HBM)
    dma = pltpu.SemaphoreType.DMA
    return pl.pallas_call(
        functools.partial(whole_kernel, sizes),
        out_shape=jax.ShapeDtypeStruct(states.shape, jnp.float32),
        in_specs=[hbm] * 10,
        out_specs=vmem,
        scratch_shapes=[
            pltpu.VMEM(states.shape, jnp.float32),
            pltpu.VMEM(start.shape, jnp.float32),
            pltpu.VMEM((1, HD), jnp.float32),
            pltpu.VMEM((1, HD), jnp.float32),
            pltpu.SMEM(step_index.shape, jnp.int32),
            pltpu.SMEM(coef_table.shape, jnp.float32),
            pltpu.SMEM(coef_index.shape, jnp.int32),
            pltpu.VMEM((3, depth, cols), half16),
            pltpu.VMEM((mod_table.shape[0], 2 * width), jnp.float32),
            pltpu.VMEM((mod_table.shape[0], width), jnp.float32),
            pltpu.VMEM((nb, rows, depth), half16),
            pltpu.VMEM((n, rows, depth), half16),
            pltpu.VMEM((nh, nb, nb * rows * 3 * own_cols // 128, 128), half16),
            pltpu.VMEM((nh, nb, nb * rows * 3 * own_cols // 128, 128), half16),
            pltpu.VMEM((nh, nb * rows, 3 * own_cols), jnp.float32),
            pltpu.VMEM((nh // 2, nb, 2 * nb * rows * own_cols // 128, 128), half16),
            pltpu.VMEM((nb, own_cols, out_cols), half16),
            pltpu.VMEM((n, rows, out_cols), half16),
            pltpu.VMEM((n, rows, out_cols), half16),
            pltpu.VMEM((rows, width), half16),
            pltpu.VMEM((rows, width), half16),
            pltpu.VMEM((local_heads, length, HD), half16),
            pltpu.VMEM((local_heads, length, HD), half16),
            pltpu.VMEM((local_heads, length, HD), half16),
            dma((11,)),
            dma((nb,)), dma((nb,)),
            dma((2 * n,)), dma((n,)),
            dma((n,)), dma((n,)),
            dma((nb * nh // 2,)), dma((nb * nh // 2,)),
            dma((2 * nb,)), dma((2 * nb,)),
            dma((2 * nb,)), dma((2 * nb,)),
            dma((n,)), dma((n,)),
            dma((nb,)), dma((nb,)),
        ],
        compiler_params=pltpu.CompilerParams(
            collective_id=0, has_side_effects=True, vmem_limit_bytes=56 * 1024 * 1024
        ),
        name="picard_step",
    )(
        states, start, jnp.transpose(w_qkv, (1, 0, 2)), w_out,
        q_gain[None], k_gain[None], mod_table, step_index, coef_table, coef_index,
    )


def on_device(sizes, *arrays):
    step_count, nh, nb = sizes
    states, start, w_qkv, w_out = arrays[:4]
    rows, width = start.shape
    depth, _, cols = w_qkv.shape
    fits = (
        step_count == 2
        and states.shape[0] == 1
        and nh % 2 == 0
        and nh & (nh - 1) == 0
        and rows % 16 == 0
        and cols % (nb * HD) == 0
        and w_out.shape[0] == cols // nb
        and (cols // nb) % 64 == 0
        and depth * nb == width
        and depth % 128 == 0
    )
    if fits:
        return one_kernel((nh, nb), *arrays)
    return general_plan(*arrays)


def solution(mesh):
    in_specs = (
        P("step", ("head", "blk"), None),
        P(("head", "blk"), None),
        P("blk", None, "head"),
        P(("head", "blk"), None),
        P(),
        P(),
        P(),
        P("step"),
        P(),
        P("step"),
    )
    out_specs = P("step", ("head", "blk"), None)
    sizes = (mesh.shape["step"], mesh.shape["head"], mesh.shape["blk"])
    return jax.shard_map(
        functools.partial(on_device, sizes), mesh=mesh, in_specs=in_specs, out_specs=out_specs, check_vma=False
    )
```
